256 devices in a mesh: region: 8 (over x, core), slab: 32 (over y, z).
Axes of the slice: x: 4, y: 4, z: 8, core: 2. Of those that a mesh axis runs over, the one named last changes fastest.
Arguments:
- waveforms: bfloat16 [16384, 48, 128], P(('region', 'slab')), may hold values from -21 to 21, as said below
- neighbours: int32 [16384, 32], P(('region', 'slab')), may hold values from 0 to 16383, as said below
- masks: int32 [16, 16384], replicated, may hold values 0 or 1
- locations: float32 [4, 16384], replicated, may hold values from -5 to 30, as said below
- stations: float32 [3, 16], replicated, may hold values from -15 to 35, as said below
Outputs:
- lag_times: float32 [16384, 512], P(('region', 'slab'))
- gradient: float32 [4, 16384], P(None, ('region', 'slab'))
The draws below stay inside these ranges and needn't reach their ends.
Inputs may be any that keep to these rules, and one draw needn't show every extreme that they name: `waveforms`: event amplitudes differ from event to event. `neighbours`: columns 0 to 23 name other events of the same device's block of 64 events. The next 6 columns name events on other devices of the same region; of the 384 such references of one device at most 25 lie on any one device, and exactly 25 on some device. Column 30 names an event at the same slab index in the region one index lower (one higher for region 0); the last column one at the same slab index in the region one index higher (one lower for the last region). `locations`: depths lie between 5 and 15. `stations`: depths lie between -1.5 and 0.
All inputs are finite; a program needn't handle non-finite values.
Results may differ from the reference program's by a relative error of at most 0.002.
Values may be sent and summed in bfloat16 or wider, within the bound.
No kernel may reach another device: no remote copies, remote signals or barrier semaphores. Data moves between devices by JAX's collectives and lax.ppermute only.
A program may use at most 128 MiB of HBM per device.

```python
import math
import jax
import jax.numpy as jnp
from jax import lax

EV_DEV = 64
STATIONS = 16
NSAMP = 128
K_LOCAL = 24
K_REGION = 6
CHANNELS = 48
NEIGHBOURS = 32
EVENTS = 16384
CAP = 25
N_REGION = 8
N_SLAB = 32


def smooth_taps(values, width):
    extent = 3 * width
    offsets = list(range(-extent, extent + 1))
    tap_weights = [math.exp(-(offset * offset) / (2.0 * width * width)) for offset in offsets]
    normaliser = math.sqrt(sum((weight * weight for weight in tap_weights)))
    summed = jnp.zeros_like(values)
    for offset, weight in zip(offsets, tap_weights):
        summed = summed + weight / normaliser * jnp.roll(values, offset, axis=-1)
    return summed


def draw_waveforms(key, part):
    key = jax.random.fold_in(key, 11)
    subkeys = jax.random.split(key, 7)
    template = smooth_taps(jax.random.truncated_normal(subkeys[0], -4.0, 4.0, (CHANNELS, NSAMP), jnp.float32), 3)
    regional = smooth_taps(jax.random.truncated_normal(subkeys[4], -4.0, 4.0, (N_REGION, CHANNELS, NSAMP), jnp.float32), 3)
    region_of = jnp.arange(EVENTS, dtype=jnp.int32) // (EVENTS // N_REGION)
    base_signal = template[None] + 0.6 * jnp.take(regional, region_of, axis=0)
    amplitude = jnp.exp(jax.random.uniform(subkeys[1], (EVENTS, 1, 1), jnp.float32, math.log(0.3), math.log(3.0)))
    noise = jax.random.truncated_normal(subkeys[2], -4.0, 4.0, (EVENTS, CHANNELS, NSAMP), jnp.float32)
    own_part = smooth_taps(jax.random.truncated_normal(subkeys[5], -4.0, 4.0, (EVENTS, CHANNELS, NSAMP), jnp.float32), 2)
    extent = max(NSAMP // 10, 1)
    whole_delay = jax.random.randint(subkeys[3], (EVENTS, STATIONS, 1), -extent, extent)
    whole_delay = jnp.repeat(whole_delay, 3, axis=1)
    fraction = jax.random.uniform(subkeys[6], (EVENTS, STATIONS, 1), jnp.float32)
    fraction = jnp.repeat(fraction, 3, axis=1)
    positions = jnp.arange(NSAMP, dtype=jnp.int32)[None, None, :]
    first_source = (positions - whole_delay) % NSAMP
    second_source = (positions - whole_delay - 1) % NSAMP
    shifted = (1.0 - fraction) * jnp.take_along_axis(base_signal, first_source, axis=2)
    shifted = shifted + fraction * jnp.take_along_axis(base_signal, second_source, axis=2)
    signal = (shifted + 0.5 * own_part) / math.sqrt(1.61)
    values = amplitude * (signal + 0.3 * noise)
    return jnp.clip(values, -21.0, 21.0).astype(jnp.bfloat16)


def draw_neighbours(key, part):
    key = jax.random.fold_in(key, 23)
    subkeys = jax.random.split(key, 6)
    devices = N_REGION * N_SLAB
    region_ids = jnp.arange(N_REGION, dtype=jnp.int32)[:, None, None]
    slab_ids = jnp.arange(N_SLAB, dtype=jnp.int32)[None, :, None]
    block_start = (region_ids * N_SLAB + slab_ids) * EV_DEV
    own_local = jnp.arange(EV_DEV, dtype=jnp.int32)[None, None, :, None]
    offset_step = jax.random.randint(subkeys[0], (N_REGION, N_SLAB, EV_DEV, K_LOCAL), 1, EV_DEV)
    local_cols = block_start[..., None] + (own_local + offset_step) % EV_DEV
    ref_count = EV_DEV * K_REGION
    busy_slab = jax.random.randint(subkeys[1], (N_REGION, 1), 0, N_SLAB)
    slab_grid = jnp.arange(N_SLAB, dtype=jnp.int32)[None, :]
    forced = jnp.where(slab_grid == busy_slab, (busy_slab + 1) % N_SLAB, busy_slab)
    slab_order = jnp.arange(N_SLAB, dtype=jnp.int32)[None, None, :]
    excluded = (slab_order == slab_grid[..., None]) | (slab_order == forced[..., None])
    ranking = excluded.astype(jnp.int32) * N_SLAB + slab_order
    allowed = jnp.argsort(ranking, axis=2, stable=True)[..., :N_SLAB - 2].astype(jnp.int32)
    slot_count = (N_SLAB - 2) * CAP
    slot_keys = jax.random.split(subkeys[2], devices)
    chosen_slots = jax.vmap(lambda subkey: jax.random.permutation(subkey, slot_count)[:ref_count - CAP])(slot_keys)
    chosen_slots = chosen_slots.reshape(N_REGION, N_SLAB, ref_count - CAP).astype(jnp.int32)
    chosen = jnp.take_along_axis(allowed, chosen_slots // CAP, axis=2)
    destination = jnp.concatenate([jnp.broadcast_to(forced[..., None], (N_REGION, N_SLAB, CAP)), chosen], axis=2)
    order_keys = jax.random.split(subkeys[3], devices)
    shuffle = jax.vmap(lambda subkey: jax.random.permutation(subkey, ref_count))(order_keys)
    shuffle = shuffle.reshape(N_REGION, N_SLAB, ref_count).astype(jnp.int32)
    destination = jnp.take_along_axis(destination, shuffle, axis=2)
    local_choice = jax.random.randint(subkeys[4], (N_REGION, N_SLAB, ref_count), 0, EV_DEV)
    region_cols = ((region_ids * N_SLAB + destination) * EV_DEV + local_choice).reshape(N_REGION, N_SLAB, EV_DEV, K_REGION)
    lower_region = jnp.where(region_ids == 0, 1, region_ids - 1)
    upper_region = jnp.where(region_ids == N_REGION - 1, N_REGION - 2, region_ids + 1)
    cross_choice = jax.random.randint(subkeys[5], (N_REGION, N_SLAB, EV_DEV, 2), 0, EV_DEV)
    lower_cols = ((lower_region * N_SLAB + slab_ids) * EV_DEV)[..., None] + cross_choice[..., :1]
    upper_cols = ((upper_region * N_SLAB + slab_ids) * EV_DEV)[..., None] + cross_choice[..., 1:]
    result = jnp.concatenate([local_cols, region_cols, lower_cols, upper_cols], axis=3)
    return result.reshape(EVENTS, NEIGHBOURS).astype(jnp.int32)


def draw_locations(key, part):
    key = jax.random.fold_in(key, 37)
    unit = jax.random.uniform(key, (4, EVENTS), jnp.float32)
    lower_ends = jnp.array([0.0, 0.0, 5.0, -4.0], jnp.float32)[:, None]
    upper_ends = jnp.array([20.0, 20.0, 12.0, 4.0], jnp.float32)[:, None]
    return lower_ends + (upper_ends - lower_ends) * unit


def draw_stations(key, part):
    key = jax.random.fold_in(key, 41)
    unit = jax.random.uniform(key, (3, STATIONS), jnp.float32)
    lower_ends = jnp.array([-10.0, -10.0, -1.0], jnp.float32)[:, None]
    upper_ends = jnp.array([30.0, 30.0, 0.0], jnp.float32)[:, None]
    return lower_ends + (upper_ends - lower_ends) * unit


def place_ends(values, stream_key, low, high):
    spot = [jax.random.randint(jax.random.fold_in(stream_key, axis), (), 0, length) for axis, length in enumerate(values.shape)]
    widest = values.shape.index(max(values.shape))
    next_to = spot[:widest] + [(spot[widest] + 1) % values.shape[widest]] + spot[widest + 1:]
    return values.at[tuple(spot)].set(low).at[tuple(next_to)].set(high)


def setup_inputs(seed: int = 0) -> dict:
    keys = jax.random.split(jax.random.key(seed), 6)
    return {
        "waveforms": draw_waveforms(jax.random.fold_in(keys[5], 71), 0),
        "neighbours": draw_neighbours(jax.random.fold_in(keys[5], 71), 0),
        "masks": place_ends((jax.random.randint(keys[2], (STATIONS, EVENTS), 0, 4) < 3).astype(jnp.int32), jax.random.fold_in(keys[2], 1), 0, 1),
        "locations": draw_locations(jax.random.fold_in(keys[5], 71), 0),
        "stations": draw_stations(jax.random.fold_in(keys[5], 71), 0),
    }


SHARPNESS = 0.1
WAVE_SPEED = 0.6

def forward_table(samples):
    half_length = samples // 2
    sample_ids = jnp.arange(samples, dtype=jnp.int32)[:, None]
    cos_bins = jnp.arange(half_length + 1, dtype=jnp.int32)[None, :]
    sin_bins = jnp.arange(1, half_length, dtype=jnp.int32)[None, :]
    cos_angle = 2.0 * jnp.pi / samples * (sample_ids * cos_bins % samples).astype(jnp.float32)
    sin_angle = 2.0 * jnp.pi / samples * (sample_ids * sin_bins % samples).astype(jnp.float32)
    table = jnp.concatenate([jnp.cos(cos_angle), -jnp.sin(sin_angle)], axis=1)
    return table.astype(jnp.bfloat16)

def inverse_table(samples):
    half_length = samples // 2
    cos_bins = jnp.arange(half_length + 1, dtype=jnp.int32)[:, None]
    sin_bins = jnp.arange(1, half_length, dtype=jnp.int32)[:, None]
    lag_ids = jnp.arange(samples, dtype=jnp.int32)[None, :]
    factors = jnp.where((cos_bins == 0) | (cos_bins == half_length), 1.0, 2.0).astype(jnp.float32) / samples
    cos_angle = 2.0 * jnp.pi / samples * (cos_bins * lag_ids % samples).astype(jnp.float32)
    sin_angle = 2.0 * jnp.pi / samples * (sin_bins * lag_ids % samples).astype(jnp.float32)
    upper_rows = factors * jnp.cos(cos_angle)
    lower_rows = -(2.0 / samples) * jnp.sin(sin_angle)
    return jnp.concatenate([upper_rows, lower_rows], axis=0).astype(jnp.bfloat16)

def lag_values(samples):
    lag_ids = jnp.arange(samples, dtype=jnp.int32)
    return jnp.where(lag_ids < samples // 2, lag_ids, lag_ids - samples).astype(jnp.float32)

def cross_packed(own_spec, partner):
    half_length = own_spec.shape[-1] // 2
    own_values = own_spec.astype(jnp.float32)
    other_values = partner.astype(jnp.float32)
    own_real = own_values[..., :half_length + 1]
    own_imag = own_values[..., half_length + 1:]
    other_real = other_values[..., :half_length + 1]
    other_imag = other_values[..., half_length + 1:]
    imag_product = own_imag * other_imag
    widths = [(0, 0)] * (imag_product.ndim - 1) + [(1, 1)]
    real_part = own_real * other_real + jnp.pad(imag_product, widths)
    imag_part = own_real[..., 1:half_length] * other_imag - own_imag * other_real[..., 1:half_length]
    return jnp.concatenate([real_part, imag_part], axis=-1).astype(jnp.bfloat16)

def soft_lags(own_spec, partner, inverse):
    crossed = cross_packed(own_spec, partner)
    layout = crossed.shape
    correlation = jnp.dot(crossed.reshape(-1, layout[-1]), inverse, preferred_element_type=jnp.float32)
    correlation = correlation.reshape(layout[:-2] + (layout[-2] // 3, 3, layout[-1]))
    scores = SHARPNESS * lax.optimization_barrier(jnp.sum(correlation, axis=-2))
    weights = jax.nn.softmax(scores, axis=-1)
    return lax.optimization_barrier(jnp.sum(weights * lag_values(layout[-1]), axis=-1))

def geometry(places, stations):
    offsets = places[:3, :, None] - stations[:, None, :]
    distance = jnp.sqrt(lax.optimization_barrier(jnp.sum(offsets * offsets, axis=0)))
    arrival = places[3][:, None] + distance / WAVE_SPEED
    direction = offsets / (WAVE_SPEED * distance)
    return (arrival, direction)

def reference(waveforms, neighbours, masks, locations, stations):
    events_all, channels, samples = waveforms.shape
    neighbour_count = neighbours.shape[1]
    station_count = stations.shape[1]
    spectra = jnp.dot(waveforms.reshape(-1, samples), forward_table(samples), preferred_element_type=jnp.float32)
    spectra = spectra.astype(jnp.bfloat16).reshape(events_all, channels, samples)
    inverse = inverse_table(samples)
    block_count = events_all // EV_DEV

    def pair_block(block):
        own_spec, partner_ids = block
        partner = jnp.take(spectra, partner_ids.reshape(-1), axis=0).reshape(EV_DEV, neighbour_count, channels, samples)
        return soft_lags(own_spec[:, None], partner, inverse)
    lag_times = lax.map(pair_block, (spectra.reshape(block_count, EV_DEV, channels, samples), neighbours.reshape(block_count, EV_DEV, neighbour_count)))
    lag_times = lag_times.reshape(events_all, neighbour_count, station_count)
    arrival, direction = geometry(locations, stations)
    mask_values = masks.astype(jnp.float32).T
    part_arrival = jnp.take(arrival, neighbours, axis=0)
    part_mask = jnp.take(mask_values, neighbours, axis=0)
    residual = mask_values[:, None, :] * part_mask * (lag_times - (part_arrival - arrival[:, None, :])) / (neighbour_count * station_count)
    own_sum = lax.optimization_barrier(jnp.sum(residual, axis=1))
    own_grad = jnp.concatenate([lax.optimization_barrier(jnp.sum(direction * own_sum[None], axis=2)), lax.optimization_barrier(jnp.sum(own_sum, axis=1))[None]], axis=0)
    part_dir = jnp.take(direction, neighbours, axis=1)
    part_grad = jnp.concatenate([lax.optimization_barrier(jnp.sum(part_dir * residual[None], axis=3)), lax.optimization_barrier(jnp.sum(residual, axis=2))[None]], axis=0)
    collected = jax.ops.segment_sum(part_grad.reshape(4, -1).T, neighbours.reshape(-1), num_segments=events_all)
    gradient = own_grad - collected.T
    return (lag_times.reshape(events_all, neighbour_count * station_count), gradient)
```

```python
import functools

import jax
import jax.numpy as jnp
import ml_dtypes
import numpy as np
from jax import lax
from jax.experimental import pallas as pl
from jax.experimental.pallas import tpu as pltpu
from jax.sharding import PartitionSpec as P

K_LOCAL = 24
K_REGION = 6
K_CROSS = 2
K_HOME = K_LOCAL + K_CROSS
COMPONENTS = 3
LANES = 128

SHARPNESS = 0.1
WAVE_SPEED = 0.6
EXPONENT_SCALE = SHARPNESS * 1.4426950408889634

F32 = jnp.float32
BF16 = jnp.bfloat16
BY_LAST = (((1,), (1,)), ((), ()))
VMEM_BYTES = 56 * 1024 * 1024


def forward_table(samples):
    half_length = samples // 2
    sample_ids = np.arange(samples)[:, None]
    cos_bins = np.arange(half_length + 1)[None, :]
    sin_bins = np.arange(1, half_length)[None, :]
    cos_angle = 2.0 * np.pi / samples * (sample_ids * cos_bins % samples)
    sin_angle = 2.0 * np.pi / samples * (sample_ids * sin_bins % samples)
    table = np.concatenate([np.cos(cos_angle), -np.sin(sin_angle)], axis=1)
    return table.astype(np.float32).astype(ml_dtypes.bfloat16)


def inverse_table(samples):
    half_length = samples // 2
    cos_bins = np.arange(half_length + 1)[:, None]
    sin_bins = np.arange(1, half_length)[:, None]
    lag_ids = np.arange(samples)[None, :]
    factors = np.where((cos_bins == 0) | (cos_bins == half_length), 1.0, 2.0) / samples
    cos_angle = 2.0 * np.pi / samples * (cos_bins * lag_ids % samples)
    sin_angle = 2.0 * np.pi / samples * (sin_bins * lag_ids % samples)
    table = np.concatenate(
        [factors * np.cos(cos_angle), -(2.0 / samples) * np.sin(sin_angle)], axis=0
    )
    return table.astype(np.float32).astype(ml_dtypes.bfloat16)


def inverse_rows(samples):
    table = inverse_table(samples).T
    real, imag = table[:, : samples // 2], table[:, samples // 2 :]
    return np.concatenate([real, real, imag, imag, table], axis=1)


def lag_values(samples):
    lag_ids = np.arange(samples)
    values = np.where(lag_ids < samples // 2, lag_ids, lag_ids - samples)
    return np.broadcast_to(values[:, None], (samples, LANES)).astype(np.float32)


def arrange(first, second):
    half = first.shape[-1] // 2
    lane = lax.broadcasted_iota(jnp.int32, first.shape, first.ndim - 1)
    real = jnp.where(lane < half, first, pltpu.roll(second, half, second.ndim - 1))
    imag = jnp.where(lane < half, pltpu.roll(first, half, first.ndim - 1), second)
    return real, imag


def swapped(spec):
    return pltpu.roll(spec, spec.shape[-1] // 2, spec.ndim - 1)


def multipliers(real, imag, packed):
    half = packed.shape[-1] // 2
    lane = lax.broadcasted_iota(jnp.int32, packed.shape, packed.ndim - 1)
    edge = (lane == 0) | (lane == half)
    turned = swapped(packed)
    packed_real = jnp.where(lane <= half, packed, turned)
    packed_imag = jnp.where(edge, 0.0, jnp.where(lane < half, turned, -packed))
    return real, jnp.where(edge, imag, real), jnp.where(edge, 0.0, imag), packed_real, packed_imag


def cross(own, partner):
    real, real_edge, imag, packed_real, packed_imag = own
    other_real, other_imag, other, other_swapped = partner
    return (
        real * other_real + imag * other_imag,
        real_edge * other_imag - imag * other_real,
        packed_real * other + packed_imag * other_swapped,
    )


def soft_lags(crossed, inverse, values):
    corr = lax.dot_general(inverse, crossed, BY_LAST, preferred_element_type=F32)
    top = jnp.max(corr, axis=0, keepdims=True)
    weights = jnp.exp2((corr - top) * EXPONENT_SCALE)
    total = jnp.sum(weights, axis=0, keepdims=True)
    moment = jnp.sum(weights * values, axis=0, keepdims=True)
    return moment / total


def two_parts(x):
    high = x.astype(BF16)
    return high, (x - high.astype(F32)).astype(BF16)


def transform(wave_ref, table_ref, scr):
    block = 384

    def step(k, carry):
        rows = pl.ds(pl.multiple_of(k * block, block), block)
        spec = jnp.dot(wave_ref[rows, :], table_ref[...], preferred_element_type=F32)
        scr[rows, :] = spec.astype(BF16).astype(F32)
        return carry

    lax.fori_loop(0, wave_ref.shape[0] // block, step, 0)


def payload_kernel(wave_ref, table_ref, ids_ref, out_ref, scr):
    stations = out_ref.shape[0] // 2
    events = ids_ref.shape[0]
    part = events // 2
    channels = stations * COMPONENTS
    transform(wave_ref, table_ref, scr)
    for s in range(stations):
        first, second, third = (
            scr[pl.ds(COMPONENTS * s + c, events, stride=channels), :] for c in range(COMPONENTS)
        )
        for k, rows in enumerate((*arrange(first, second), third)):
            rows = rows.astype(BF16)
            out_ref[s, k * events : (k + 1) * events, :] = rows
            out_ref[stations + s, k * events : (k + 1) * events, :] = rows
    ids = ids_ref[...].T[K_LOCAL : K_LOCAL + K_REGION]
    tail = out_ref.shape[1] - COMPONENTS * events
    for h in range(2):
        mine = ids[:, h * part : (h + 1) * part]
        row = jnp.concatenate([mine[n : n + 1] for n in range(K_REGION)], axis=1)
        row = jnp.concatenate([row, jnp.zeros((1, 2 * LANES - row.shape[1]), jnp.int32)], axis=1)
        source, event = row // events % (2 * stations), row % events
        rows = jnp.concatenate(
            [source[:, :LANES], source[:, LANES:], event[:, :LANES], event[:, LANES:]]
            + [jnp.zeros((tail - 4, LANES), jnp.int32)],
            axis=0,
        )
        rows = rows.astype(F32).astype(BF16)
        for s in range(stations):
            out_ref[h * stations + s, COMPONENTS * events :, :] = rows


def by_event_kernel(wave_ref, table_ref, out_ref, scr):
    events, _, stations, _ = out_ref.shape
    channels = stations * COMPONENTS
    transform(wave_ref, table_ref, scr)

    def one_event(event, carry):
        first, second, third = (
            scr[pl.ds(event * channels + c, stations, stride=COMPONENTS), :]
            for c in range(COMPONENTS)
        )
        for k, rows in enumerate((*arrange(first, second), third)):
            out_ref[event, k] = rows.astype(BF16)
        return carry

    lax.fori_loop(0, events, one_event, 0, unroll=4)


BATCH = 4


def home_kernel(
    pool_ids,
    id_row_ref,
    low_ref,
    own_ref,
    high_ref,
    partner_ref,
    pick_ref,
    inverse_ref,
    values_ref,
    arrival_ref,
    mask_ref,
    lag_ref,
    sums_ref,
    to_low_ref,
    to_high_ref,
    pool,
    crossed,
    partner_rows,
    residuals,
    spread,
    sems,
):
    events = own_ref.shape[0]
    stations = own_ref.shape[2]
    width = K_HOME * stations
    copies = [
        pltpu.make_async_copy(
            ref, pool.at[pl.ds(k * events, events), pl.ds(0, COMPONENTS)], sems.at[k]
        )
        for k, ref in enumerate((low_ref, own_ref, high_ref))
    ]
    for copy in copies:
        copy.start()
    for copy in copies:
        copy.wait()

    def swap(event, carry):
        pool[event, COMPONENTS] = swapped(pool[event, COMPONENTS - 1].astype(F32)).astype(BF16)
        return carry

    lax.fori_loop(0, 3 * events, swap, 0, unroll=8)
    values = jnp.tile(values_ref[...], (1, BATCH * width // LANES))

    def some_events(step, carry):
        for b in range(BATCH):
            event = step * BATCH + b
            own = multipliers(*(pool[events + event, k].astype(F32) for k in range(COMPONENTS)))
            for n in range(K_HOME):
                j = pool_ids[event * K_HOME + n]
                partner = [pool[j, k].astype(F32) for k in range(COMPONENTS + 1)]
                rows = slice(b * width + n * stations, b * width + (n + 1) * stations)
                for k, values_k in enumerate(cross(own, partner)):
                    crossed[rows, k * LANES : (k + 1) * LANES] = values_k.astype(BF16)
                partner_rows[rows, :] = partner_ref[j]
        lags = soft_lags(crossed[...], inverse_ref[...], values)
        picks = lax.dot_general(
            pick_ref[...], partner_rows[...], BY_LAST, preferred_element_type=F32
        )
        for b in range(BATCH):
            row = pl.ds(step * BATCH + b, 1)
            lag = lags[:, b * width : (b + 1) * width]
            picked = picks[:, b * width : (b + 1) * width]
            local = K_LOCAL * stations
            gap = jnp.zeros((1, K_REGION * stations), F32)
            lag_ref[row, :] = jnp.concatenate([lag[:, :local], gap, lag[:, local:]], axis=1)
            residuals[row, :] = (
                mask_ref[row, :]
                * picked[1:2]
                * (lag - (picked[0:1] - arrival_ref[row, :]))
                * (1.0 / lag_ref.shape[1])
            )
        return carry

    lax.fori_loop(0, events // BATCH, some_events, 0)

    residual = residuals[...]
    column = lax.broadcasted_iota(jnp.int32, (events, width), 1) // stations
    for n in range(K_HOME):
        high, low = two_parts(jnp.where(column == n, residual, 0.0))
        spread[n * events : (n + 1) * events, :width] = high
        spread[n * events : (n + 1) * events, width:] = low
    pool_rows = lax.broadcasted_iota(jnp.int32, (3 * events, K_HOME * events), 0)
    hits = jnp.where(id_row_ref[...] == pool_rows, 1.0, 0.0).astype(BF16)
    gathered = jnp.dot(hits, spread[...], preferred_element_type=F32)
    gathered = gathered[:, :width] + gathered[:, width:]
    station = lax.broadcasted_iota(jnp.int32, (stations, width), 0)
    lane = lax.broadcasted_iota(jnp.int32, (stations, width), 1) % stations
    fold = jnp.where(station == lane, 1.0, 0.0)
    fold_dot = functools.partial(
        lax.dot_general,
        dimension_numbers=BY_LAST,
        precision=lax.Precision.HIGHEST,
        preferred_element_type=F32,
    )
    own_sums = fold_dot(fold, residual)
    low_sums = fold_dot(fold, gathered[:events])
    in_sums = fold_dot(fold, gathered[events : 2 * events])
    high_sums = fold_dot(fold, gathered[2 * events :])
    sums_ref[...] = own_sums - in_sums
    to_low_ref[...] = low_sums
    to_high_ref[...] = high_sums


def task_kernel(
    half_ref,
    spec_ref,
    tables_ref,
    arrival_ref,
    mask_ref,
    inverse_ref,
    values_ref,
    home_ref,
    out_ref,
    table,
    fetched,
    crossed,
    id_rows,
    ids,
    sem,
):
    sources, payload, _ = spec_ref.shape
    events = tables_ref.shape[0] // 4
    part = events // 2
    span = K_REGION * part
    width = 2 * span
    half = half_ref[0]

    def read_ids(source, carry):
        tail = spec_ref[source, COMPONENTS * events :, :].astype(F32)
        rows = (tail[:2] * events + tail[2:4]).astype(jnp.int32)
        id_rows[pl.ds(2 * source, 1), :] = rows[:1]
        id_rows[pl.ds(2 * source + 1, 1), :] = rows[1:]
        return carry

    lax.fori_loop(0, sources, read_ids, 0)
    copy = pltpu.make_async_copy(id_rows, ids, sem)
    copy.start()

    def fill(source, carry):
        rows = [
            spec_ref[source, k * events : (k + 1) * events, :].astype(F32)
            for k in range(COMPONENTS)
        ]
        rows.append(swapped(rows[-1]))
        base = source * (events * 8)
        for k, values_k in enumerate(rows):
            table[pl.ds(base + k, events, stride=8), :] = values_k
            table[pl.ds(base + 4 + k, events, stride=8), :] = values_k
        return carry

    lax.fori_loop(0, sources, fill, 0)
    copy.wait()

    values = jnp.tile(values_ref[...], (1, width // LANES))
    upper = lax.broadcasted_iota(jnp.int32, (8, LANES), 0) < 4
    source_rows = lax.broadcasted_iota(jnp.int32, (sources, width), 0)
    event_rows = lax.broadcasted_iota(jnp.int32, (events, width), 0)
    lane = lax.broadcasted_iota(jnp.int32, (1, width), 1)
    out_lane = lax.broadcasted_iota(jnp.int32, (1, LANES), 1)
    own_event = lane % part + half * part

    def two_sources(step, sums):
        for q in range(0, width, 2):
            row, column = q // span * 2 + q % span // LANES, q % span % LANES
            first = ids[step * 4 + row, column]
            second = ids[step * 4 + row, column + 1]
            first = table[pl.ds(pl.multiple_of(first * 8, 8), 8), :]
            second = table[pl.ds(pl.multiple_of(second * 8, 8), 8), :]
            fetched[q * 4 : q * 4 + 8, :] = jnp.where(upper, first, second)
        for u in range(2):
            own = multipliers(
                *(
                    spec_ref[
                        2 * step + u,
                        pl.ds(pl.multiple_of(k * events + half * part, part), part),
                        :,
                    ].astype(F32)
                    for k in range(COMPONENTS)
                )
            )
            for n in range(K_REGION):
                start = u * span + n * part
                partner = [
                    fetched[pl.ds(start * 4 + k, part, stride=4), :]
                    for k in range(COMPONENTS + 1)
                ]
                for k, values_k in enumerate(cross(own, partner)):
                    crossed[start : start + part, k * LANES : (k + 1) * LANES] = values_k.astype(
                        BF16
                    )
        lag = soft_lags(crossed[...], inverse_ref[...], values)
        out_ref[2 * step, :, :LANES] = lag[:, :LANES]
        out_ref[2 * step + 1, :, :LANES] = lag[:, span : span + LANES]
        for u in range(2):
            rest = lag[:, u * span + LANES : (u + 1) * span]
            out_ref[2 * step + u, :, LANES : LANES + rest.shape[1]] = rest
        id_row = jnp.concatenate(
            [
                piece
                for u in range(2)
                for piece in (
                    id_rows[pl.ds(4 * step + 2 * u, 1), :],
                    id_rows[pl.ds(4 * step + 2 * u + 1, 1), :][:, : span - LANES],
                )
            ],
            axis=1,
        )
        from_source = source_rows == id_row // events
        from_event = event_rows == id_row % events
        looked_up = jnp.dot(
            tables_ref[...],
            jnp.where(from_source, 1.0, 0.0).astype(BF16),
            preferred_element_type=F32,
        )
        arrival = looked_up[:events] + looked_up[events : 2 * events]
        arrival = arrival + looked_up[2 * events : 3 * events]
        arrival = jnp.sum(jnp.where(from_event, arrival, 0.0), axis=0, keepdims=True)
        mask = jnp.where(from_event, looked_up[3 * events :], 0.0)
        mask = jnp.sum(mask, axis=0, keepdims=True)
        row = pl.ds(step, 1)
        residual = (
            mask_ref[row, :]
            * mask
            * (lag - (arrival - arrival_ref[row, :]))
            * (1.0 / ((K_HOME + K_REGION) * (sources // 2)))
        )
        own_source = lane // span + 2 * step
        for sign, by_source, by_event in (
            (-1.0, from_source, from_event),
            (1.0, source_rows == own_source, event_rows == own_event),
        ):
            high, low = two_parts(jnp.where(by_source, sign * residual, 0.0))
            where_event = jnp.where(by_event, 1.0, 0.0).astype(BF16)
            for term in (high, low):
                sums = sums + lax.dot_general(
                    term, where_event, BY_LAST, preferred_element_type=F32
                )
        return sums

    sums = lax.fori_loop(0, sources // 2, two_sources, jnp.zeros((sources, events), F32))
    out_ref[:, 0, span:] = sums


def final_kernel(
    remote_ref, lag_in_ref, sums_ref, low_ref, high_ref, place_ref, stations_ref, lag_ref, grad_ref
):
    events = lag_ref.shape[0]
    stations = sums_ref.shape[0]
    part = events // 2
    span = K_REGION * part
    lag_ref[...] = lag_in_ref[...]
    for h in range(2):
        turned = remote_ref[h * stations : (h + 1) * stations, 0, :span].T
        for n in range(K_REGION):
            start = (K_LOCAL + n) * stations
            lag_ref[h * part : (h + 1) * part, start : start + stations] = turned[
                n * part : (n + 1) * part
            ]
    sums = sums_ref[...] - low_ref[...] - high_ref[...]
    sums = sums + remote_ref[:stations, 0, span:] + remote_ref[stations:, 0, span:]
    offsets = [place_ref[c : c + 1, :] - stations_ref[:, c : c + 1] for c in range(3)]
    distance = jnp.sqrt(sum(offset * offset for offset in offsets))
    for c in range(3):
        direction = offsets[c] / (WAVE_SPEED * distance)
        grad_ref[c : c + 1, :] = jnp.sum(direction * sums, axis=0, keepdims=True)
    grad_ref[3:4, :] = jnp.sum(sums, axis=0, keepdims=True)


def arrivals(places, stations):
    offsets = places[:3, :, None] - stations[:, None, :]
    distance = jnp.sqrt(jnp.sum(offsets * offsets, axis=0))
    return places[3][:, None] + distance / WAVE_SPEED


def three_parts(x):
    high = lax.reduce_precision(x, 8, 7)
    middle = lax.reduce_precision(x - high, 8, 7)
    low = x - high - middle
    return high, middle, low


def vmem(count):
    return [pl.BlockSpec(memory_space=pltpu.VMEM)] * count


def shape(dims, dtype=F32):
    return jax.ShapeDtypeStruct(dims, dtype)


def shifted(block, axis, distance):
    devices = range(lax.axis_size(axis))
    route = [(i - distance, i) for i in devices if i - distance in devices]
    return lax.ppermute(block, axis, route)


def per_device(waveforms, neighbours, masks, locations, stations):
    events, channels, samples = waveforms.shape
    neighbour_count = neighbours.shape[1]
    station_count = stations.shape[1]
    slab_count = lax.axis_size("slab")
    region_events = slab_count * events
    region_index = lax.axis_index("region")
    slab_index = lax.axis_index("slab")
    block_start = region_index * region_events + slab_index * events
    half = slab_index // station_count
    my_station = slab_index % station_count
    part = events // 2
    span = K_REGION * part
    params = pltpu.CompilerParams(vmem_limit_bytes=VMEM_BYTES)
    inverse = jnp.asarray(inverse_rows(samples))
    values = jnp.asarray(lag_values(samples))

    wave_rows = waveforms.reshape(-1, samples)
    table = jnp.asarray(forward_table(samples))
    payload = pl.pallas_call(
        payload_kernel,
        out_shape=shape((2 * station_count, COMPONENTS * events + 8, samples), BF16),
        in_specs=vmem(3),
        out_specs=vmem(1)[0],
        scratch_shapes=[pltpu.VMEM((events * channels, samples), F32)],
        compiler_params=params,
        name="payload",
    )(wave_rows, table, neighbours)
    task_spec = lax.all_to_all(payload, "slab", 0, 0, tiled=True)
    by_event = pl.pallas_call(
        by_event_kernel,
        out_shape=shape((events, COMPONENTS, station_count, samples), BF16),
        in_specs=vmem(2),
        out_specs=vmem(1)[0],
        scratch_shapes=[pltpu.VMEM((events * channels, samples), F32)],
        compiler_params=params,
        name="by_event",
    )(wave_rows, table)
    low_spec = shifted(by_event, "region", 1)
    high_spec = shifted(by_event, "region", -1)

    starts = [
        jnp.clip(region_index + k, 0, lax.axis_size("region") - 1) * region_events
        + slab_index * events
        for k in (-1, 0, 1)
    ]
    near_places = jnp.concatenate(
        [lax.dynamic_slice_in_dim(locations, start, events, 1) for start in starts], axis=1
    )
    near_masks = jnp.concatenate(
        [lax.dynamic_slice_in_dim(masks, start, events, 1) for start in starts], axis=1
    ).astype(F32)
    near_arrival = arrivals(near_places, stations)
    partner_rows = jnp.stack([*three_parts(near_arrival), near_masks.T], axis=-1).astype(BF16)
    partner_rows = jnp.pad(partner_rows, ((0, 0), (0, 0), (0, LANES - 4)))
    pick = np.zeros((8, LANES), ml_dtypes.bfloat16)
    pick[0, :3] = 1
    pick[1, 3] = 1
    own_places = near_places[:, events : 2 * events]
    own_arrival = jnp.tile(near_arrival[events : 2 * events], (1, K_HOME))
    own_mask = jnp.tile(near_masks[:, events : 2 * events].T, (1, K_HOME))
    cross_ids = neighbours[:, K_LOCAL + K_REGION :]
    lower_side = cross_ids // region_events < region_index
    pool_ids = jnp.concatenate(
        [
            events + neighbours[:, :K_LOCAL] % events,
            jnp.where(lower_side, 0, 2 * events) + cross_ids % events,
        ],
        axis=1,
    )
    width = K_HOME * station_count
    lag_home, sums, to_low, to_high = pl.pallas_call(
        home_kernel,
        out_shape=(
            shape((events, neighbour_count * station_count)),
            shape((station_count, events)),
            shape((station_count, events)),
            shape((station_count, events)),
        ),
        in_specs=[pl.BlockSpec(memory_space=pltpu.SMEM)]
        + vmem(1)
        + [pl.BlockSpec(memory_space=pl.ANY)] * 3
        + vmem(6),
        out_specs=vmem(4),
        scratch_shapes=[
            pltpu.VMEM((3 * events, COMPONENTS + 1, station_count, samples), BF16),
            pltpu.VMEM((BATCH * width, COMPONENTS * samples), BF16),
            pltpu.VMEM((BATCH * width, LANES), BF16),
            pltpu.VMEM((events, width), F32),
            pltpu.VMEM((K_HOME * events, 2 * width), BF16),
            pltpu.SemaphoreType.DMA((3,)),
        ],
        compiler_params=params,
        cost_estimate=pl.CostEstimate(flops=10**10, bytes_accessed=10**7, transcendentals=10**7),
        name="home",
    )(
        pool_ids.reshape(-1),
        pool_ids.T.reshape(1, -1),
        low_spec,
        by_event,
        high_spec,
        partner_rows,
        jnp.asarray(pick),
        inverse,
        values,
        own_arrival,
        own_mask,
    )
    from_high = shifted(to_low, "region", -1)
    from_low = shifted(to_high, "region", 1)

    region_places = lax.dynamic_slice_in_dim(
        locations, region_index * region_events, region_events, 1
    )
    station_place = lax.dynamic_slice_in_dim(stations, my_station, 1, 1)
    task_arrival = arrivals(region_places, station_place)[:, 0].reshape(slab_count, events)
    task_mask = (
        lax.dynamic_slice(
            masks, (my_station, region_index * region_events), (1, region_events)
        )
        .reshape(slab_count, events)
        .astype(F32)
    )
    tables = jnp.concatenate([*three_parts(task_arrival), task_mask], axis=1).T.astype(BF16)

    def per_pair(rows):
        rows = lax.dynamic_slice_in_dim(rows, half * part, part, 1)
        return jnp.tile(rows, (1, K_REGION)).reshape(slab_count // 2, 2 * span)

    results = pl.pallas_call(
        task_kernel,
        out_shape=shape((slab_count, 1, span + events)),
        in_specs=[pl.BlockSpec(memory_space=pltpu.SMEM)] + vmem(6)
        + [pl.BlockSpec(memory_space=pl.ANY)],
        out_specs=vmem(1)[0],
        scratch_shapes=[
            pltpu.VMEM((region_events * 8, LANES), F32),
            pltpu.VMEM((2 * span * 4, LANES), F32),
            pltpu.VMEM((2 * span, COMPONENTS * samples), BF16),
            pltpu.VMEM((2 * slab_count, LANES), jnp.int32),
            pltpu.SMEM((2 * slab_count, LANES), jnp.int32),
            pltpu.SemaphoreType.DMA,
        ],
        compiler_params=params,
        cost_estimate=pl.CostEstimate(flops=10**10, bytes_accessed=10**7, transcendentals=10**7),
        name="task",
    )(
        half.reshape(1),
        task_spec,
        tables,
        per_pair(task_arrival),
        per_pair(task_mask),
        inverse,
        values,
        sums,
    )
    remote = lax.all_to_all(results, "slab", 0, 0, tiled=True)
    return pl.pallas_call(
        final_kernel,
        out_shape=(
            shape((events, neighbour_count * station_count)),
            shape((4, events)),
        ),
        in_specs=vmem(7),
        out_specs=vmem(2),
        compiler_params=params,
        name="final",
    )(remote, lag_home, sums, from_low, from_high, own_places, stations.T)


def solution(mesh):
    in_specs = (P(("region", "slab"), None, None), P(("region", "slab"), None), P(), P(), P())
    out_specs = (P(("region", "slab"), None), P(None, ("region", "slab")))
    return jax.shard_map(
        per_device, mesh=mesh, in_specs=in_specs, out_specs=out_specs, check_vma=False
    )
```

```python
import functools

import jax
import jax.numpy as jnp
import ml_dtypes
import numpy as np
from jax import lax
from jax.experimental import pallas as pl
from jax.experimental.pallas import tpu as pltpu
from jax.sharding import PartitionSpec as P

K_LOCAL = 24
K_REGION = 6
K_CROSS = 2
K_HOME = K_LOCAL + K_CROSS
COMPONENTS = 3
BATCH = 4
LANES = 128

SHARPNESS = 0.1
WAVE_SPEED = 0.6
EXPONENT_SCALE = SHARPNESS * 1.4426950408889634

F32 = jnp.float32
BF16 = jnp.bfloat16
BY_LAST = (((1,), (1,)), ((), ()))


def forward_table(samples):
    half_length = samples // 2
    sample_ids = np.arange(samples)[:, None]
    cos_bins = np.arange(half_length + 1)[None, :]
    sin_bins = np.arange(1, half_length)[None, :]
    cos_angle = 2.0 * np.pi / samples * (sample_ids * cos_bins % samples)
    sin_angle = 2.0 * np.pi / samples * (sample_ids * sin_bins % samples)
    table = np.concatenate([np.cos(cos_angle), -np.sin(sin_angle)], axis=1)
    return table.astype(np.float32).astype(ml_dtypes.bfloat16)


def inverse_table(samples):
    half_length = samples // 2
    cos_bins = np.arange(half_length + 1)[:, None]
    sin_bins = np.arange(1, half_length)[:, None]
    lag_ids = np.arange(samples)[None, :]
    factors = np.where((cos_bins == 0) | (cos_bins == half_length), 1.0, 2.0) / samples
    cos_angle = 2.0 * np.pi / samples * (cos_bins * lag_ids % samples)
    sin_angle = 2.0 * np.pi / samples * (sin_bins * lag_ids % samples)
    table = np.concatenate(
        [factors * np.cos(cos_angle), -(2.0 / samples) * np.sin(sin_angle)], axis=0
    )
    return table.astype(np.float32).astype(ml_dtypes.bfloat16)


def inverse_rows(samples):
    table = inverse_table(samples)
    real, imag = table[: samples // 2], table[samples // 2 :]
    return np.concatenate([real, real, imag, imag, table], axis=0)


def lag_values(samples):
    lag_ids = np.arange(samples)
    values = np.where(lag_ids < samples // 2, lag_ids, lag_ids - samples)
    return np.broadcast_to(values[:, None], (samples, LANES)).astype(np.float32)


def arrange(first, second):
    half = first.shape[-1] // 2
    lane = lax.broadcasted_iota(jnp.int32, first.shape, first.ndim - 1)
    real = jnp.where(lane < half, first, pltpu.roll(second, half, second.ndim - 1))
    imag = jnp.where(lane < half, pltpu.roll(first, half, first.ndim - 1), second)
    return real, imag


def swapped(spec):
    return pltpu.roll(spec, spec.shape[-1] // 2, spec.ndim - 1)


def multipliers(real, imag, packed):
    half = packed.shape[-1] // 2
    lane = lax.broadcasted_iota(jnp.int32, packed.shape, packed.ndim - 1)
    edge = (lane == 0) | (lane == half)
    turned = swapped(packed)
    packed_real = jnp.where(lane <= half, packed, turned)
    packed_imag = jnp.where(edge, 0.0, jnp.where(lane < half, turned, -packed))
    return real, jnp.where(edge, imag, real), jnp.where(edge, 0.0, imag), packed_real, packed_imag


def cross(own, partner):
    real, real_edge, imag, packed_real, packed_imag = own
    other_real, other_imag, other, other_swapped = partner
    return (
        real * other_real + imag * other_imag,
        real_edge * other_imag - imag * other_real,
        packed_real * other + packed_imag * other_swapped,
    )


def soft_lags(corr, values):
    corr = corr.T
    top = jnp.max(corr, axis=0, keepdims=True)
    weights = jnp.exp2((corr - top) * EXPONENT_SCALE)
    total = jnp.sum(weights, axis=0, keepdims=True)
    moment = jnp.sum(weights * values, axis=0, keepdims=True)
    return moment / total


def all_soft_lags(crossed_ref, inverse_ref, values_ref, block):
    inverse, values = inverse_ref[...], values_ref[...]
    lags = []
    for start in range(0, crossed_ref.shape[0], block):
        corr = jnp.dot(
            crossed_ref[start : start + block, :], inverse, preferred_element_type=F32
        )
        for k in range(0, block, LANES):
            lags.append(soft_lags(corr[k : k + LANES], values))
    return jnp.concatenate(lags, axis=1)


def two_parts(x):
    high = x.astype(BF16)
    return high, (x - high.astype(F32)).astype(BF16)


def transform(wave_ref, table_ref, scr):
    block = 384

    def step(k, carry):
        rows = pl.ds(pl.multiple_of(k * block, block), block)
        spec = jnp.dot(wave_ref[rows, :], table_ref[...], preferred_element_type=F32)
        scr[rows, :] = spec.astype(BF16).astype(F32)
        return carry

    lax.fori_loop(0, wave_ref.shape[0] // block, step, 0, unroll=True)


def near_columns(ref, window, sem, region):
    slab = lax.axis_index("slab")
    start = region * (lax.axis_size("slab") * LANES // 2) + slab // 2 * LANES
    copy = pltpu.make_async_copy(
        ref.at[:, pl.ds(pl.multiple_of(start, LANES), LANES)], window, sem
    )
    copy.start()
    return copy


def own_columns(window):
    odd = lax.axis_index("slab") % 2 == 1
    values = window[...].astype(F32)
    half = values.shape[1] // 2
    return jnp.where(odd, pltpu.roll(values, half, 1), values)[:, :half]


def travel(places, station_columns):
    offsets = [places[c : c + 1, :] - station_columns[:, c : c + 1] for c in range(3)]
    return offsets, jnp.sqrt(sum(offset * offset for offset in offsets))


def three_parts(x):
    high = x.astype(BF16)
    rest = x - high.astype(F32)
    middle = rest.astype(BF16)
    return high, middle, (rest - middle.astype(F32)).astype(BF16)


def put_crossed(crossed, rows, own, partner):
    for k, values in enumerate(cross(own, partner)):
        crossed[rows, k * LANES : (k + 1) * LANES] = values.astype(BF16)


def look_up(arrival, mask, hits):
    stations = arrival.shape[0]
    rows = jnp.concatenate([p.astype(F32) for p in three_parts(arrival)] + [mask], axis=0)
    rows = jnp.dot(rows.astype(BF16), hits, preferred_element_type=F32)
    high, middle, low, found = (rows[k * stations : (k + 1) * stations] for k in range(4))
    return high + middle + low, found


def sum_by_name(residual, hits):
    stations = residual.shape[0]
    parts = jnp.concatenate(two_parts(residual), axis=0)
    sums = lax.dot_general(parts, hits, BY_LAST, preferred_element_type=F32)
    return sums[:stations] + sums[stations:]


def by_pair(lags, columns):
    turned = lags.T
    stations = turned.shape[0] // columns
    return jnp.concatenate(
        [turned[n * stations : (n + 1) * stations] for n in range(columns)], axis=1
    )


def payload_kernel(wave_ref, table_ref, ids_ref, kept_ref, sent_ref, by_event_ref, scr):
    stations = sent_ref.shape[0]
    events = ids_ref.shape[1]
    part = events // 2
    channels = stations * COMPONENTS
    core = lax.axis_index("region") % 2
    transform(wave_ref, table_ref, scr)
    ids = ids_ref[K_LOCAL : K_LOCAL + K_REGION, :]
    tail = sent_ref.shape[1] - COMPONENTS * part
    for out, base, half in ((kept_ref, core * stations, core), (sent_ref, 0, 1 - core)):
        mine = jnp.where(half == 1, ids[:, part:], ids[:, :part])
        row = jnp.concatenate([mine[n : n + 1] for n in range(K_REGION)], axis=1)
        row = jnp.concatenate([row, jnp.zeros((1, 2 * LANES - row.shape[1]), jnp.int32)], axis=1)
        source, event = row // events % (2 * stations), row % events
        rows = jnp.concatenate(
            [source[:, :LANES], source[:, LANES:], event[:, :LANES], event[:, LANES:]]
            + [jnp.zeros((tail - 4, LANES), jnp.int32)],
            axis=0,
        )
        rows = rows.astype(F32).astype(BF16)
        for s in range(stations):
            first, second, third = (
                scr[pl.ds(half * (part * channels) + COMPONENTS * s + c, part, stride=channels), :]
                for c in range(COMPONENTS)
            )
            for k, values in enumerate((*arrange(first, second), third)):
                out[base + s, k * part : (k + 1) * part, :] = values.astype(BF16)
            out[base + s, COMPONENTS * part :, :] = rows

    def one_event(event, carry):
        first, second, third = (
            scr[pl.ds(event * channels + c, stations, stride=COMPONENTS), :]
            for c in range(COMPONENTS)
        )
        for k, values in enumerate((*arrange(first, second), third, swapped(third))):
            by_event_ref[event, k] = values.astype(BF16)
        return carry

    lax.fori_loop(0, events, one_event, 0, unroll=8)


def home_kernel(
    ids,
    id_ref,
    stations_ref,
    inverse_ref,
    values_ref,
    core_ref,
    own_ref,
    x_ref,
    locations_ref,
    masks_ref,
    order_ref,
    lag_ref,
    sums_ref,
    to_core_ref,
    to_x_ref,
    done_ref,
    raw,
    pool,
    crossed,
    hits,
    place_windows,
    mask_windows,
    sems,
):
    events, _, stations, _ = own_ref.shape
    width = K_HOME * stations
    batches = events // BATCH
    region = lax.axis_index("region")
    last = lax.axis_size("region") - 1
    copies = [
        pltpu.make_async_copy(ref, raw.at[pl.ds(k * events, events)], sems.at[k])
        for k, ref in enumerate((core_ref, own_ref, x_ref))
    ]
    for copy in copies:
        copy.start()
    odd = region % 2
    near = (region + 1 - 2 * odd, region, jnp.clip(region - 1 + 2 * odd, 0, last))
    for k, where in enumerate(near):
        copies.append(near_columns(locations_ref, place_windows.at[k], sems.at[3 + k], where))
        copies.append(near_columns(masks_ref, mask_windows.at[k], sems.at[6 + k], where))
    blocks = [events] * K_LOCAL + [
        jnp.where((odd == 1) | (region == 0), 0, 2 * events),
        jnp.where((odd == 0) | (region == last), 0, 2 * events),
    ]
    columns = [*range(K_LOCAL), *range(K_LOCAL + K_REGION, K_LOCAL + K_REGION + K_CROSS)]
    named = lax.broadcasted_iota(jnp.int32, (3 * events, events), 0)
    for n in range(0, K_HOME, 2):
        pair = [
            jnp.where(
                id_ref[columns[m] : columns[m] + 1, :] % events + blocks[m] == named, 1.0, 0.0
            )
            for m in (n, n + 1)
        ]
        hits[:, n * events : (n + 2) * events] = jnp.concatenate(pair, axis=1).astype(BF16)
    done_ref[...] = jnp.zeros(done_ref.shape, done_ref.dtype)
    for copy in copies:
        copy.wait()

    def widen(event, carry):
        pool[event] = raw[event].astype(F32)
        return carry

    lax.fori_loop(0, 3 * events, widen, 0, unroll=8)

    def cross_batch(batch, rows_ref):
        for b in range(BATCH):
            event = batch * BATCH + b
            own = multipliers(*(pool[events + event, k] for k in range(COMPONENTS)))
            for n in range(K_HOME):
                j = lax.bitwise_and(ids[columns[n], event], events - 1) + blocks[n]
                partner = [pool[j, k] for k in range(COMPONENTS + 1)]
                start = b * width + n * stations
                put_crossed(rows_ref, slice(start, start + stations), own, partner)

    def finish_batch(batch, rows_ref):
        lags = all_soft_lags(rows_ref, inverse_ref, values_ref, BATCH * width)
        for b in range(BATCH):
            lag_ref[pl.ds(batch * BATCH + b, 1), :] = lags[:, b * width : (b + 1) * width]

    def two_batches(step, carry):
        cross_batch(2 * step + 1, crossed.at[1])
        finish_batch(2 * step, crossed.at[0])
        cross_batch(jnp.minimum(2 * step + 2, batches - 1), crossed.at[0])
        finish_batch(2 * step + 1, crossed.at[1])
        return carry

    cross_batch(0, crossed.at[0])
    lax.fori_loop(0, batches // 2, two_batches, 0)

    station_columns = stations_ref[...].T
    arrivals, masks = [], []
    for k in range(3):
        places = own_columns(place_windows.at[k])
        masks.append(own_columns(mask_windows.at[k]))
        _, distance = travel(places, station_columns)
        arrivals.append(places[3:4, :] + distance / WAVE_SPEED)
    near_arrivals, found = look_up(
        jnp.concatenate(arrivals, axis=1), jnp.concatenate(masks, axis=1), hits[...]
    )
    residual = (
        jnp.tile(masks[1], (1, K_HOME))
        * found
        * (by_pair(lag_ref[...], K_HOME) - (near_arrivals - jnp.tile(arrivals[1], (1, K_HOME))))
        * (1.0 / ((K_HOME + K_REGION) * stations))
    )
    own_sums = sum(residual[:, n * events : (n + 1) * events] for n in range(K_HOME))
    sums = sum_by_name(residual, hits[...])
    to_core_ref[...] = sums[:, :events]
    sums_ref[...] = own_sums - sums[:, events : 2 * events]
    to_x_ref[...] = sums[:, 2 * events :]


def task_kernel(
    stations_ref,
    mine_ref,
    other_ref,
    inverse_ref,
    values_ref,
    locations_ref,
    masks_ref,
    out_ref,
    table,
    fetched_even,
    fetched_odd,
    crossed_even,
    crossed_odd,
    id_rows,
    residuals,
    own_terms,
    place_window,
    mask_window,
    ids,
    sems,
):
    sources, payload, _ = mine_ref.shape
    stations = sources // 2
    part = payload // COMPONENTS // 8 * 8
    events = 2 * part
    span = K_REGION * part
    width = 2 * span
    region_events = sources * events
    region, slab = lax.axis_index("region"), lax.axis_index("slab")
    core = region % 2
    task_region = region - core + slab // stations
    station = slab % stations
    columns = pl.ds(pl.multiple_of(task_region * region_events, region_events), region_events)
    copies = [
        pltpu.make_async_copy(locations_ref.at[:, columns], place_window, sems.at[0]),
        pltpu.make_async_copy(masks_ref.at[:, columns], mask_window, sems.at[1]),
    ]
    for copy in copies:
        copy.start()

    def read_ids(source, carry):
        tail = mine_ref[source, COMPONENTS * part :, :].astype(F32)
        rows = ((tail[:2] * events + tail[2:4]) * 8).astype(jnp.int32)
        id_rows[pl.ds(2 * source, 1), :] = rows[:1]
        id_rows[pl.ds(2 * source + 1, 1), :] = rows[1:]
        return carry

    lax.fori_loop(0, sources, read_ids, 0, unroll=8)
    id_copy = pltpu.make_async_copy(id_rows, ids, sems.at[2])
    id_copy.start()

    def fill(source, carry):
        for ref, half in ((mine_ref, core), (other_ref, 1 - core)):
            rows = [
                ref[source, k * part : (k + 1) * part, :].astype(F32) for k in range(COMPONENTS)
            ]
            rows.append(swapped(rows[-1]))
            base = (source * events + half * part) * 8
            for k, values_k in enumerate(rows):
                table[pl.ds(base + k, part, stride=8), :] = values_k
                table[pl.ds(base + 4 + k, part, stride=8), :] = values_k
        return carry

    lax.fori_loop(0, sources, fill, 0, unroll=4)
    for copy in copies:
        copy.wait()
    offsets = [place_window[c : c + 1, :] - stations_ref[c, station] for c in range(3)]
    arrival = place_window[3:4, :] + (
        jnp.sqrt(sum(offset * offset for offset in offsets)) / WAVE_SPEED
    )
    mask = mask_window[pl.ds(station, 1), :].astype(F32)

    def as_rows(row):
        return jnp.concatenate(
            [row[:, t * LANES : (t + 1) * LANES] for t in range(region_events // LANES)], axis=0
        )

    tables = jnp.concatenate(
        [part_of.astype(F32) for part_of in three_parts(as_rows(arrival))] + [as_rows(mask)], axis=0
    ).astype(BF16)
    half_rows = tables.shape[0] // 4
    lane = lax.broadcasted_iota(jnp.int32, (LANES, width), 1)
    event_rows = lax.broadcasted_iota(jnp.int32, (LANES, width), 0)
    own_hits = event_rows == lane // span * events + core * part + lane % part
    own_hits = jnp.where(own_hits, 1.0, 0.0).astype(BF16)
    own = jnp.dot(tables, own_hits, preferred_element_type=F32)
    own_terms[:half_rows] = own[:half_rows] + own[half_rows : 2 * half_rows] + own[
        2 * half_rows : 3 * half_rows
    ]
    own_terms[half_rows:] = own[3 * half_rows :]
    id_copy.wait()

    upper = lax.broadcasted_iota(jnp.int32, (8, LANES), 0) < 4
    source_rows = lax.broadcasted_iota(jnp.int32, (half_rows, width), 0)
    out_lane = lax.broadcasted_iota(jnp.int32, (1, LANES), 1)

    def fetch(step, into):
        for q in range(0, width, 2):
            row, column = q // span * 2 + q % span // LANES, q % span % LANES
            first = ids[step * 4 + row, column]
            second = ids[step * 4 + row, column + 1]
            first = table[pl.ds(pl.multiple_of(first, 8), 8), :]
            second = table[pl.ds(pl.multiple_of(second, 8), 8), :]
            into[q * 4 : q * 4 + 8, :] = jnp.where(upper, first, second)

    def cross_two(step, source, into):
        for u in range(2):
            own = multipliers(
                *(
                    mine_ref[2 * step + u, k * part : (k + 1) * part, :].astype(F32)
                    for k in range(COMPONENTS)
                )
            )
            for n in range(K_REGION):
                start = u * span + n * part
                partner = [
                    source[pl.ds(start * 4 + k, part, stride=4), :]
                    for k in range(COMPONENTS + 1)
                ]
                put_crossed(into, slice(start, start + part), own, partner)

    def finish(step, rows_ref, sums):
        lag = all_soft_lags(rows_ref, inverse_ref, values_ref, LANES)
        for u in range(2):
            rest = lag[:, u * span + LANES : (u + 1) * span]
            rest = jnp.concatenate([rest, jnp.zeros((1, LANES - rest.shape[1]), F32)], axis=1)
            out_ref[2 * step + u] = jnp.concatenate(
                [lag[:, u * span : u * span + LANES], rest], axis=0
            )
        id_row = jnp.concatenate(
            [
                piece
                for u in range(2)
                for piece in (
                    id_rows[pl.ds(4 * step + 2 * u, 1), :],
                    id_rows[pl.ds(4 * step + 2 * u + 1, 1), :][:, : span - LANES],
                )
            ],
            axis=1,
        )
        id_row = id_row // 8
        from_source = source_rows == id_row // LANES
        from_event = jnp.where(event_rows == id_row % LANES, 1.0, 0.0).astype(BF16)
        looked_up = jnp.dot(tables, from_event, preferred_element_type=F32)
        arrival = looked_up[:half_rows] + looked_up[half_rows : 2 * half_rows]
        arrival = arrival + looked_up[2 * half_rows : 3 * half_rows]
        arrival = jnp.sum(jnp.where(from_source, arrival, 0.0), axis=0, keepdims=True)
        mask = jnp.where(from_source, looked_up[3 * half_rows :], 0.0)
        mask = jnp.sum(mask, axis=0, keepdims=True)
        residual = (
            own_terms[pl.ds(half_rows + step, 1), :]
            * mask
            * (lag - (arrival - own_terms[pl.ds(step, 1), :]))
            * (1.0 / ((K_LOCAL + K_REGION + K_CROSS) * stations))
        )
        residuals[pl.ds(step, 1), :] = residual
        terms = jnp.concatenate(two_parts(jnp.where(from_source, residual, 0.0)), axis=0)
        return sums + lax.dot_general(terms, from_event, BY_LAST, preferred_element_type=F32)

    steps = sources // 2

    def two_steps(pair, sums):
        first = 2 * pair
        fetch(jnp.minimum(first + 2, steps - 1), fetched_even)
        cross_two(first + 1, fetched_odd, crossed_odd)
        sums = finish(first, crossed_even, sums)
        fetch(jnp.minimum(first + 3, steps - 1), fetched_odd)
        cross_two(jnp.minimum(first + 2, steps - 1), fetched_even, crossed_even)
        return finish(first + 1, crossed_odd, sums)

    fetch(0, fetched_even)
    cross_two(0, fetched_even, crossed_even)
    fetch(1, fetched_odd)
    sums = lax.fori_loop(0, steps // 2, two_steps, jnp.zeros((2 * half_rows, LANES), F32))
    terms = jnp.concatenate(two_parts(residuals[...]), axis=0)
    sums = lax.dot_general(terms, own_hits, BY_LAST, preferred_element_type=F32) - sums
    sums = sums[:half_rows] + sums[half_rows:]
    for t in range(half_rows):
        for u in range(2):
            row = sums[t : t + 1, :]
            row = pltpu.roll(row, LANES // 2, 1) if u == 0 else row
            lags = out_ref[2 * t + u]
            out_ref[2 * t + u] = jnp.concatenate(
                [lags[:1], jnp.where(out_lane < span - LANES, lags[1:], row)], axis=0
            )


def gather_kernel(home_lag_ref, sums_ref, core_ref, x_ref, order_ref, lag_ref, out_ref):
    stations = sums_ref.shape[0]
    local = K_LOCAL * stations
    remote = K_REGION * stations
    home = home_lag_ref[...]
    gap = jnp.zeros((home.shape[0], remote), F32)
    lag_ref[...] = jnp.concatenate([home[:, :local], gap, home[:, local:]], axis=1)
    out_ref[...] = sums_ref[...] - core_ref[...] - x_ref[...]


def final_kernel(
    kept_ref,
    got_ref,
    home_lag_ref,
    sums_ref,
    stations_ref,
    locations_ref,
    lag_ref,
    grad_ref,
    place_window,
    lag_window,
    sems,
):
    events = grad_ref.shape[1]
    stations = sums_ref.shape[0]
    part = events // 2
    span = K_REGION * part
    core = lax.axis_index("region") % 2
    copy = near_columns(locations_ref, place_window, sems.at[0], lax.axis_index("region"))
    columns = pl.ds(K_LOCAL * stations, LANES)
    lags = pltpu.make_async_copy(home_lag_ref.at[:, columns], lag_window, sems.at[1])
    lags.start()
    sums = sums_ref[...]
    block = pl.ds(pl.multiple_of(core * stations, stations), stations)
    kept, got = kept_ref[block], got_ref[block]
    rows = []
    for h in range(2):
        values = jnp.where(core == h, kept, got)
        sums = sums + values[:, 1, span - LANES :]
        turned = jnp.concatenate([values[:, 0, :], values[:, 1, : span - LANES]], axis=1).T
        rows.append(
            jnp.concatenate([turned[n * part : (n + 1) * part] for n in range(K_REGION)], axis=1)
        )
    rows = jnp.concatenate(rows, axis=0)
    copy.wait()
    lags.wait()
    lag_window[:, : rows.shape[1]] = rows
    lags = pltpu.make_async_copy(lag_window, lag_ref.at[:, columns], sems.at[1])
    lags.start()
    offsets, distance = travel(own_columns(place_window), stations_ref[...].T)
    for c in range(3):
        direction = offsets[c] / (WAVE_SPEED * distance)
        grad_ref[c : c + 1, :] = jnp.sum(direction * sums, axis=0, keepdims=True)
    grad_ref[3:4, :] = jnp.sum(sums, axis=0, keepdims=True)
    lags.wait()


def params(mebibytes):
    return pltpu.CompilerParams(vmem_limit_bytes=mebibytes * 1024 * 1024)


def vmem(count):
    return [pl.BlockSpec(memory_space=pltpu.VMEM)] * count


def smem(count):
    return [pl.BlockSpec(memory_space=pltpu.SMEM)] * count


def anywhere(count):
    return [pl.BlockSpec(memory_space=pl.ANY)] * count


def shape(dims, dtype=F32):
    return jax.ShapeDtypeStruct(dims, dtype)


def other_core(block):
    count = lax.axis_size("region")
    return lax.ppermute(block, "region", [(i, i + 1 - 2 * (i % 2)) for i in range(count)])


def other_chip(block):
    odd = range(1, lax.axis_size("region") - 1, 2)
    return lax.ppermute(block, "region", [p for i in odd for p in ((i, i + 1), (i + 1, i))])


def per_device(waveforms, neighbours, masks, locations, stations):
    events, channels, samples = waveforms.shape
    neighbour_count = neighbours.shape[1]
    station_count = stations.shape[1]
    slab_count = lax.axis_size("slab")
    region_events = slab_count * events
    core = lax.axis_index("region") % 2
    part = events // 2
    span = K_REGION * part
    inverse = jnp.asarray(inverse_rows(samples))
    values = jnp.asarray(lag_values(samples))
    wave_rows = waveforms.reshape(-1, samples)
    table = jnp.asarray(forward_table(samples))
    id_columns = neighbours.T
    by_event_shape = (events, COMPONENTS + 1, station_count, samples)
    payload_rows = COMPONENTS * part + 8

    kept, sent, by_event = pl.pallas_call(
        payload_kernel,
        out_shape=(
            shape((slab_count, payload_rows, samples), BF16),
            shape((station_count, payload_rows, samples), BF16),
            shape(by_event_shape, BF16),
        ),
        in_specs=vmem(3),
        out_specs=vmem(3),
        scratch_shapes=[pltpu.VMEM((events * channels, samples), F32)],
        compiler_params=params(16),
        name="payload",
    )(wave_rows, table, id_columns)
    payload = lax.dynamic_update_slice_in_dim(
        kept, other_core(sent), (1 - core) * station_count, 0
    )
    mine = lax.all_to_all(payload, "slab", 0, 0, tiled=True)

    core_spec = other_core(by_event)
    x_spec = other_chip(by_event)

    width = K_HOME * station_count
    lag_home, sums, to_core, to_x, done = pl.pallas_call(
        home_kernel,
        out_shape=(
            shape((events, width)),
            shape((station_count, events)),
            shape((station_count, events)),
            shape((station_count, events)),
            shape((1, 1, LANES), BF16),
        ),
        in_specs=smem(1) + vmem(4) + anywhere(6),
        out_specs=vmem(5),
        scratch_shapes=[
            pltpu.VMEM((3 * events, *by_event_shape[1:]), BF16),
            pltpu.VMEM((3 * events, *by_event_shape[1:]), F32),
            pltpu.VMEM((2, BATCH * width, COMPONENTS * samples), BF16),
            pltpu.VMEM((3 * events, K_HOME * events), BF16),
            pltpu.VMEM((3, 4, LANES), F32),
            pltpu.VMEM((3, station_count, LANES), jnp.int32),
            pltpu.SemaphoreType.DMA((9,)),
        ],
        compiler_params=params(26),
        cost_estimate=pl.CostEstimate(flops=10**10, bytes_accessed=10**7, transcendentals=10**7),
        name="home",
    )(
        id_columns,
        id_columns,
        stations,
        inverse,
        values,
        core_spec,
        by_event,
        x_spec,
        locations,
        masks,
        payload,
    )
    from_core = other_core(to_core)
    from_x = other_chip(to_x)
    mine = lax.dynamic_update_slice(mine, done, (0, payload_rows - 1, 0))
    other = other_core(mine)

    results = pl.pallas_call(
        task_kernel,
        out_shape=shape((slab_count, 2, LANES)),
        in_specs=smem(1) + vmem(4) + anywhere(2),
        out_specs=vmem(1)[0],
        scratch_shapes=[
            pltpu.VMEM((region_events * 8, LANES), F32),
            pltpu.VMEM((2 * span * 4, LANES), F32),
            pltpu.VMEM((2 * span * 4, LANES), F32),
            pltpu.VMEM((2 * span, COMPONENTS * samples), BF16),
            pltpu.VMEM((2 * span, COMPONENTS * samples), BF16),
            pltpu.VMEM((2 * slab_count, LANES), jnp.int32),
            pltpu.VMEM((slab_count // 2, 2 * span), F32),
            pltpu.VMEM((slab_count, 2 * span), F32),
            pltpu.VMEM((4, region_events), F32),
            pltpu.VMEM((station_count, region_events), jnp.int32),
            pltpu.SMEM((2 * slab_count, LANES), jnp.int32),
            pltpu.SemaphoreType.DMA((3,)),
        ],
        compiler_params=params(26),
        cost_estimate=pl.CostEstimate(flops=10**10, bytes_accessed=10**7, transcendentals=10**7),
        name="task",
    )(stations, mine, other, inverse, values, locations, masks)
    back = lax.all_to_all(results, "slab", 0, 0, tiled=True)
    lag_home, sums = pl.pallas_call(
        gather_kernel,
        out_shape=(
            shape((events, neighbour_count * station_count)),
            shape((station_count, events)),
        ),
        in_specs=vmem(4) + anywhere(1),
        out_specs=vmem(2),
        compiler_params=params(8),
        cost_estimate=pl.CostEstimate(flops=10**9, bytes_accessed=10**7, transcendentals=0),
        name="gather",
    )(lag_home, sums, from_core, from_x, results)
    return pl.pallas_call(
        final_kernel,
        out_shape=(
            shape((events, neighbour_count * station_count)),
            shape((4, events)),
        ),
        in_specs=vmem(2) + anywhere(1) + vmem(2) + anywhere(1),
        out_specs=(anywhere(1)[0], vmem(1)[0]),
        scratch_shapes=[
            pltpu.VMEM((4, LANES), F32),
            pltpu.VMEM((events, LANES), F32),
            pltpu.SemaphoreType.DMA((2,)),
        ],
        input_output_aliases={2: 0},
        compiler_params=params(8),
        name="final",
    )(back, other_core(back), lag_home, sums, stations, locations)


def solution(mesh):
    in_specs = (P(("region", "slab"), None, None), P(("region", "slab"), None), P(), P(), P())
    out_specs = (P(("region", "slab"), None), P(None, ("region", "slab")))
    return jax.shard_map(
        per_device, mesh=mesh, in_specs=in_specs, out_specs=out_specs, check_vma=False
    )
```

```python
import functools

import jax
import jax.numpy as jnp
import ml_dtypes
import numpy as np
from jax import lax
from jax.experimental import pallas as pl
from jax.experimental.pallas import tpu as pltpu
from jax.sharding import PartitionSpec as P

K_LOCAL = 24
K_REGION = 6
K_CROSS = 2
K_HOME = K_LOCAL + K_CROSS
COMPONENTS = 3
BATCH = 4
LANES = 128

SHARPNESS = 0.1
WAVE_SPEED = 0.6
EXPONENT_SCALE = SHARPNESS * 1.4426950408889634

F32 = jnp.float32
BF16 = jnp.bfloat16
BY_LAST = (((1,), (1,)), ((), ()))


def forward_table(samples):
    half_length = samples // 2
    sample_ids = np.arange(samples)[:, None]
    cos_bins = np.arange(half_length + 1)[None, :]
    sin_bins = np.arange(1, half_length)[None, :]
    cos_angle = 2.0 * np.pi / samples * (sample_ids * cos_bins % samples)
    sin_angle = 2.0 * np.pi / samples * (sample_ids * sin_bins % samples)
    table = np.concatenate([np.cos(cos_angle), -np.sin(sin_angle)], axis=1)
    return table.astype(np.float32).astype(ml_dtypes.bfloat16)


def inverse_table(samples):
    half_length = samples // 2
    cos_bins = np.arange(half_length + 1)[:, None]
    sin_bins = np.arange(1, half_length)[:, None]
    lag_ids = np.arange(samples)[None, :]
    factors = np.where((cos_bins == 0) | (cos_bins == half_length), 1.0, 2.0) / samples
    cos_angle = 2.0 * np.pi / samples * (cos_bins * lag_ids % samples)
    sin_angle = 2.0 * np.pi / samples * (sin_bins * lag_ids % samples)
    table = np.concatenate(
        [factors * np.cos(cos_angle), -(2.0 / samples) * np.sin(sin_angle)], axis=0
    )
    return table.astype(np.float32).astype(ml_dtypes.bfloat16)


def inverse_rows(samples):
    table = inverse_table(samples)
    real, imag = table[: samples // 2], table[samples // 2 :]
    return np.concatenate([real, real, imag, imag, table], axis=0)


def lag_values(samples):
    lag_ids = np.arange(samples)
    values = np.where(lag_ids < samples // 2, lag_ids, lag_ids - samples)
    return np.broadcast_to(values[:, None], (samples, LANES)).astype(np.float32)


def arrange(first, second):
    half = first.shape[-1] // 2
    lane = lax.broadcasted_iota(jnp.int32, first.shape, first.ndim - 1)
    real = jnp.where(lane < half, first, pltpu.roll(second, half, second.ndim - 1))
    imag = jnp.where(lane < half, pltpu.roll(first, half, first.ndim - 1), second)
    return real, imag


def swapped(spec):
    return pltpu.roll(spec, spec.shape[-1] // 2, spec.ndim - 1)


def multipliers(real, imag, packed):
    half = packed.shape[-1] // 2
    lane = lax.broadcasted_iota(jnp.int32, packed.shape, packed.ndim - 1)
    edge = (lane == 0) | (lane == half)
    turned = swapped(packed)
    packed_real = jnp.where(lane <= half, packed, turned)
    packed_imag = jnp.where(edge, 0.0, jnp.where(lane < half, turned, -packed))
    return real, jnp.where(edge, imag, real), jnp.where(edge, 0.0, imag), packed_real, packed_imag


def cross(own, partner):
    real, real_edge, imag, packed_real, packed_imag = own
    other_real, other_imag, other, other_swapped = partner
    return (
        real * other_real + imag * other_imag,
        real_edge * other_imag - imag * other_real,
        packed_real * other + packed_imag * other_swapped,
    )


def soft_lags(corr, values):
    corr = corr.T
    top = jnp.max(corr, axis=0, keepdims=True)
    weights = jnp.exp2((corr - top) * EXPONENT_SCALE)
    total = jnp.sum(weights, axis=0, keepdims=True)
    moment = jnp.sum(weights * values, axis=0, keepdims=True)
    return moment / total


def all_soft_lags(crossed_ref, inverse_ref, values_ref, block):
    inverse, values = inverse_ref[...], values_ref[...]
    lags = []
    for start in range(0, crossed_ref.shape[0], block):
        corr = jnp.dot(
            crossed_ref[start : start + block, :], inverse, preferred_element_type=F32
        )
        for k in range(0, block, LANES):
            lags.append(soft_lags(corr[k : k + LANES], values))
    return jnp.concatenate(lags, axis=1)


def two_parts(x):
    high = x.astype(BF16)
    return high, (x - high.astype(F32)).astype(BF16)


def transform(wave_ref, table_ref, scr):
    block = 384

    def step(k, carry):
        rows = pl.ds(pl.multiple_of(k * block, block), block)
        spec = jnp.dot(wave_ref[rows, :], table_ref[...], preferred_element_type=F32)
        scr[rows, :] = spec.astype(BF16).astype(F32)
        return carry

    lax.fori_loop(0, wave_ref.shape[0] // block, step, 0, unroll=True)


def near_columns(ref, window, sem, region):
    slab = lax.axis_index("slab")
    start = region * (lax.axis_size("slab") * LANES // 2) + slab // 2 * LANES
    copy = pltpu.make_async_copy(
        ref.at[:, pl.ds(pl.multiple_of(start, LANES), LANES)], window, sem
    )
    copy.start()
    return copy


def own_columns(window):
    odd = lax.axis_index("slab") % 2 == 1
    values = window[...].astype(F32)
    half = values.shape[1] // 2
    return jnp.where(odd, pltpu.roll(values, half, 1), values)[:, :half]


def travel(places, station_columns):
    offsets = [places[c : c + 1, :] - station_columns[:, c : c + 1] for c in range(3)]
    return offsets, jnp.sqrt(sum(offset * offset for offset in offsets))


def three_parts(x):
    high = x.astype(BF16)
    rest = x - high.astype(F32)
    middle = rest.astype(BF16)
    return high, middle, (rest - middle.astype(F32)).astype(BF16)


def put_crossed(crossed, rows, own, partner):
    for k, values in enumerate(cross(own, partner)):
        crossed[rows, k * LANES : (k + 1) * LANES] = values.astype(BF16)


def look_up(arrival, mask, hits):
    stations = arrival.shape[0]
    rows = jnp.concatenate([p.astype(F32) for p in three_parts(arrival)] + [mask], axis=0)
    rows = jnp.dot(rows.astype(BF16), hits, preferred_element_type=F32)
    high, middle, low, found = (rows[k * stations : (k + 1) * stations] for k in range(4))
    return high + middle + low, found


def sum_by_name(residual, hits):
    stations = residual.shape[0]
    parts = jnp.concatenate(two_parts(residual), axis=0)
    sums = lax.dot_general(parts, hits, BY_LAST, preferred_element_type=F32)
    return sums[:stations] + sums[stations:]


def by_pair(lags, columns):
    turned = lags.T
    stations = turned.shape[0] // columns
    return jnp.concatenate(
        [turned[n * stations : (n + 1) * stations] for n in range(columns)], axis=1
    )


def payload_kernel(wave_ref, table_ref, ids_ref, kept_ref, sent_ref, by_event_ref, scr):
    stations = sent_ref.shape[0]
    events = ids_ref.shape[1]
    part = events // 2
    channels = stations * COMPONENTS
    core = lax.axis_index("region") % 2
    transform(wave_ref, table_ref, scr)
    ids = ids_ref[K_LOCAL : K_LOCAL + K_REGION, :]
    tail = sent_ref.shape[1] - COMPONENTS * part
    for out, base, half in ((kept_ref, core * stations, core), (sent_ref, 0, 1 - core)):
        mine = jnp.where(half == 1, ids[:, part:], ids[:, :part])
        row = jnp.concatenate([mine[n : n + 1] for n in range(K_REGION)], axis=1)
        row = jnp.concatenate([row, jnp.zeros((1, 2 * LANES - row.shape[1]), jnp.int32)], axis=1)
        source, event = row // events % (2 * stations), row % events
        rows = jnp.concatenate(
            [source[:, :LANES], source[:, LANES:], event[:, :LANES], event[:, LANES:]]
            + [jnp.zeros((tail - 4, LANES), jnp.int32)],
            axis=0,
        )
        rows = rows.astype(F32).astype(BF16)
        for s in range(stations):
            first, second, third = (
                scr[pl.ds(half * (part * channels) + COMPONENTS * s + c, part, stride=channels), :]
                for c in range(COMPONENTS)
            )
            for k, values in enumerate((*arrange(first, second), third)):
                out[base + s, k * part : (k + 1) * part, :] = values.astype(BF16)
            out[base + s, COMPONENTS * part :, :] = rows

    def one_event(event, carry):
        first, second, third = (
            scr[pl.ds(event * channels + c, stations, stride=COMPONENTS), :]
            for c in range(COMPONENTS)
        )
        for k, values in enumerate((*arrange(first, second), third, swapped(third))):
            by_event_ref[event, k] = values.astype(BF16)
        return carry

    lax.fori_loop(0, events, one_event, 0, unroll=8)


def home_kernel(
    ids,
    id_ref,
    stations_ref,
    inverse_ref,
    values_ref,
    core_ref,
    own_ref,
    x_ref,
    locations_ref,
    masks_ref,
    lag_ref,
    sums_ref,
    to_core_ref,
    to_x_ref,
    done_ref,
    raw,
    pool,
    crossed,
    hits,
    place_windows,
    mask_windows,
    sems,
):
    events, _, stations, _ = own_ref.shape
    width = K_HOME * stations
    batches = events // BATCH
    region = lax.axis_index("region")
    last = lax.axis_size("region") - 1
    copies = [
        pltpu.make_async_copy(ref, raw.at[pl.ds(k * events, events)], sems.at[k])
        for k, ref in enumerate((core_ref, own_ref, x_ref))
    ]
    for copy in copies:
        copy.start()
    odd = region % 2
    near = (region + 1 - 2 * odd, region, jnp.clip(region - 1 + 2 * odd, 0, last))
    for k, where in enumerate(near):
        copies.append(near_columns(locations_ref, place_windows.at[k], sems.at[3 + k], where))
        copies.append(near_columns(masks_ref, mask_windows.at[k], sems.at[6 + k], where))
    blocks = [events] * K_LOCAL + [
        jnp.where((odd == 1) | (region == 0), 0, 2 * events),
        jnp.where((odd == 0) | (region == last), 0, 2 * events),
    ]
    columns = [*range(K_LOCAL), *range(K_LOCAL + K_REGION, K_LOCAL + K_REGION + K_CROSS)]
    named = lax.broadcasted_iota(jnp.int32, (3 * events, events), 0)
    for n in range(0, K_HOME, 2):
        pair = [
            jnp.where(
                id_ref[columns[m] : columns[m] + 1, :] % events + blocks[m] == named, 1.0, 0.0
            )
            for m in (n, n + 1)
        ]
        hits[:, n * events : (n + 2) * events] = jnp.concatenate(pair, axis=1).astype(BF16)
    done_ref[...] = jnp.zeros(done_ref.shape, done_ref.dtype)
    for copy in copies:
        copy.wait()

    def widen(event, carry):
        pool[event] = raw[event].astype(F32)
        return carry

    lax.fori_loop(0, 3 * events, widen, 0, unroll=8)

    def cross_batch(batch, rows_ref):
        for b in range(BATCH):
            event = batch * BATCH + b
            own = multipliers(*(pool[events + event, k] for k in range(COMPONENTS)))
            for n in range(K_HOME):
                j = lax.bitwise_and(ids[columns[n], event], events - 1) + blocks[n]
                partner = [pool[j, k] for k in range(COMPONENTS + 1)]
                start = b * width + n * stations
                put_crossed(rows_ref, slice(start, start + stations), own, partner)

    def finish_batch(batch, rows_ref):
        lags = all_soft_lags(rows_ref, inverse_ref, values_ref, BATCH * width)
        for b in range(BATCH):
            lag_ref[pl.ds(batch * BATCH + b, 1), :] = lags[:, b * width : (b + 1) * width]

    def two_batches(step, carry):
        cross_batch(2 * step + 1, crossed.at[1])
        finish_batch(2 * step, crossed.at[0])
        cross_batch(jnp.minimum(2 * step + 2, batches - 1), crossed.at[0])
        finish_batch(2 * step + 1, crossed.at[1])
        return carry

    cross_batch(0, crossed.at[0])
    lax.fori_loop(0, batches // 2, two_batches, 0)

    station_columns = stations_ref[...].T
    arrivals, masks = [], []
    for k in range(3):
        places = own_columns(place_windows.at[k])
        masks.append(own_columns(mask_windows.at[k]))
        _, distance = travel(places, station_columns)
        arrivals.append(places[3:4, :] + distance / WAVE_SPEED)
    near_arrivals, found = look_up(
        jnp.concatenate(arrivals, axis=1), jnp.concatenate(masks, axis=1), hits[...]
    )
    residual = (
        jnp.tile(masks[1], (1, K_HOME))
        * found
        * (by_pair(lag_ref[...], K_HOME) - (near_arrivals - jnp.tile(arrivals[1], (1, K_HOME))))
        * (1.0 / ((K_HOME + K_REGION) * stations))
    )
    own_sums = sum(residual[:, n * events : (n + 1) * events] for n in range(K_HOME))
    sums = sum_by_name(residual, hits[...])
    to_core_ref[...] = sums[:, :events]
    sums_ref[...] = own_sums - sums[:, events : 2 * events]
    to_x_ref[...] = sums[:, 2 * events :]


def task_kernel(
    stations_ref,
    mine_ref,
    other_ref,
    inverse_ref,
    values_ref,
    locations_ref,
    masks_ref,
    out_ref,
    table,
    fetched_even,
    fetched_odd,
    crossed_even,
    crossed_odd,
    id_rows,
    residuals,
    own_terms,
    place_window,
    mask_window,
    ids,
    sems,
):
    sources, payload, _ = mine_ref.shape
    stations = sources // 2
    part = payload // COMPONENTS // 8 * 8
    events = 2 * part
    span = K_REGION * part
    width = 2 * span
    region_events = sources * events
    region, slab = lax.axis_index("region"), lax.axis_index("slab")
    core = region % 2
    task_region = region - core + slab // stations
    station = slab % stations
    columns = pl.ds(pl.multiple_of(task_region * region_events, region_events), region_events)
    copies = [
        pltpu.make_async_copy(locations_ref.at[:, columns], place_window, sems.at[0]),
        pltpu.make_async_copy(masks_ref.at[:, columns], mask_window, sems.at[1]),
    ]
    for copy in copies:
        copy.start()

    def read_ids(source, carry):
        tail = mine_ref[source, COMPONENTS * part :, :].astype(F32)
        rows = ((tail[:2] * events + tail[2:4]) * 8).astype(jnp.int32)
        id_rows[pl.ds(2 * source, 1), :] = rows[:1]
        id_rows[pl.ds(2 * source + 1, 1), :] = rows[1:]
        return carry

    lax.fori_loop(0, sources, read_ids, 0, unroll=8)
    id_copy = pltpu.make_async_copy(id_rows, ids, sems.at[2])
    id_copy.start()

    def fill(source, carry):
        for ref, half in ((mine_ref, core), (other_ref, 1 - core)):
            rows = [
                ref[source, k * part : (k + 1) * part, :].astype(F32) for k in range(COMPONENTS)
            ]
            rows.append(swapped(rows[-1]))
            base = (source * events + half * part) * 8
            for k, values_k in enumerate(rows):
                table[pl.ds(base + k, part, stride=8), :] = values_k
                table[pl.ds(base + 4 + k, part, stride=8), :] = values_k
        return carry

    lax.fori_loop(0, sources, fill, 0, unroll=4)
    for copy in copies:
        copy.wait()
    offsets = [place_window[c : c + 1, :] - stations_ref[c, station] for c in range(3)]
    arrival = place_window[3:4, :] + (
        jnp.sqrt(sum(offset * offset for offset in offsets)) / WAVE_SPEED
    )
    mask = mask_window[pl.ds(station, 1), :].astype(F32)

    def as_rows(row):
        return jnp.concatenate(
            [row[:, t * LANES : (t + 1) * LANES] for t in range(region_events // LANES)], axis=0
        )

    tables = jnp.concatenate(
        [part_of.astype(F32) for part_of in three_parts(as_rows(arrival))] + [as_rows(mask)], axis=0
    ).astype(BF16)
    half_rows = tables.shape[0] // 4
    lane = lax.broadcasted_iota(jnp.int32, (LANES, width), 1)
    event_rows = lax.broadcasted_iota(jnp.int32, (LANES, width), 0)
    own_hits = event_rows == lane // span * events + core * part + lane % part
    own_hits = jnp.where(own_hits, 1.0, 0.0).astype(BF16)
    own = jnp.dot(tables, own_hits, preferred_element_type=F32)
    own_terms[:half_rows] = own[:half_rows] + own[half_rows : 2 * half_rows] + own[
        2 * half_rows : 3 * half_rows
    ]
    own_terms[half_rows:] = own[3 * half_rows :]
    id_copy.wait()

    upper = lax.broadcasted_iota(jnp.int32, (8, LANES), 0) < 4
    source_rows = lax.broadcasted_iota(jnp.int32, (half_rows, width), 0)
    out_lane = lax.broadcasted_iota(jnp.int32, (1, LANES), 1)

    def fetch(step, into):
        for q in range(0, width, 2):
            row, column = q // span * 2 + q % span // LANES, q % span % LANES
            first = ids[step * 4 + row, column]
            second = ids[step * 4 + row, column + 1]
            first = table[pl.ds(pl.multiple_of(first, 8), 8), :]
            second = table[pl.ds(pl.multiple_of(second, 8), 8), :]
            into[q * 4 : q * 4 + 8, :] = jnp.where(upper, first, second)

    def cross_two(step, source, into):
        for u in range(2):
            own = multipliers(
                *(
                    mine_ref[2 * step + u, k * part : (k + 1) * part, :].astype(F32)
                    for k in range(COMPONENTS)
                )
            )
            for n in range(K_REGION):
                start = u * span + n * part
                partner = [
                    source[pl.ds(start * 4 + k, part, stride=4), :]
                    for k in range(COMPONENTS + 1)
                ]
                put_crossed(into, slice(start, start + part), own, partner)

    def finish(step, rows_ref, sums):
        lag = all_soft_lags(rows_ref, inverse_ref, values_ref, LANES)
        for u in range(2):
            rest = lag[:, u * span + LANES : (u + 1) * span]
            rest = jnp.concatenate([rest, jnp.zeros((1, LANES - rest.shape[1]), F32)], axis=1)
            out_ref[2 * step + u] = jnp.concatenate(
                [lag[:, u * span : u * span + LANES], rest], axis=0
            )
        id_row = jnp.concatenate(
            [
                piece
                for u in range(2)
                for piece in (
                    id_rows[pl.ds(4 * step + 2 * u, 1), :],
                    id_rows[pl.ds(4 * step + 2 * u + 1, 1), :][:, : span - LANES],
                )
            ],
            axis=1,
        )
        id_row = id_row // 8
        from_source = source_rows == id_row // LANES
        from_event = jnp.where(event_rows == id_row % LANES, 1.0, 0.0).astype(BF16)
        looked_up = jnp.dot(tables, from_event, preferred_element_type=F32)
        arrival = looked_up[:half_rows] + looked_up[half_rows : 2 * half_rows]
        arrival = arrival + looked_up[2 * half_rows : 3 * half_rows]
        arrival = jnp.sum(jnp.where(from_source, arrival, 0.0), axis=0, keepdims=True)
        mask = jnp.where(from_source, looked_up[3 * half_rows :], 0.0)
        mask = jnp.sum(mask, axis=0, keepdims=True)
        residual = (
            own_terms[pl.ds(half_rows + step, 1), :]
            * mask
            * (lag - (arrival - own_terms[pl.ds(step, 1), :]))
            * (1.0 / ((K_LOCAL + K_REGION + K_CROSS) * stations))
        )
        residuals[pl.ds(step, 1), :] = residual
        terms = jnp.concatenate(two_parts(jnp.where(from_source, residual, 0.0)), axis=0)
        return sums + lax.dot_general(terms, from_event, BY_LAST, preferred_element_type=F32)

    steps = sources // 2

    def two_steps(pair, sums):
        first = 2 * pair
        fetch(jnp.minimum(first + 2, steps - 1), fetched_even)
        cross_two(first + 1, fetched_odd, crossed_odd)
        sums = finish(first, crossed_even, sums)
        fetch(jnp.minimum(first + 3, steps - 1), fetched_odd)
        cross_two(jnp.minimum(first + 2, steps - 1), fetched_even, crossed_even)
        return finish(first + 1, crossed_odd, sums)

    fetch(0, fetched_even)
    cross_two(0, fetched_even, crossed_even)
    fetch(1, fetched_odd)
    sums = lax.fori_loop(0, steps // 2, two_steps, jnp.zeros((2 * half_rows, LANES), F32))
    terms = jnp.concatenate(two_parts(residuals[...]), axis=0)
    sums = lax.dot_general(terms, own_hits, BY_LAST, preferred_element_type=F32) - sums
    sums = sums[:half_rows] + sums[half_rows:]
    for t in range(half_rows):
        for u in range(2):
            row = sums[t : t + 1, :]
            row = pltpu.roll(row, LANES // 2, 1) if u == 0 else row
            lags = out_ref[2 * t + u]
            out_ref[2 * t + u] = jnp.concatenate(
                [lags[:1], jnp.where(out_lane < span - LANES, lags[1:], row)], axis=0
            )


def gather_kernel(
    home_lag_ref,
    sums_ref,
    core_ref,
    x_ref,
    stations_ref,
    locations_ref,
    order_ref,
    lag_ref,
    last_ref,
    out_ref,
    direction_ref,
    place_window,
    sem,
):
    stations, events = sums_ref.shape
    copy = near_columns(locations_ref, place_window, sem, lax.axis_index("region"))
    local = K_LOCAL * stations
    remote = K_REGION * stations
    home = home_lag_ref[...]
    gap = jnp.zeros((events, remote), F32)
    last = jnp.concatenate([gap, home[:, local:]], axis=1)
    last_ref[...] = last
    lag_ref[...] = jnp.concatenate([home[:, :local], last], axis=1)
    out_ref[...] = sums_ref[...] - core_ref[...] - x_ref[...]
    copy.wait()
    offsets, distance = travel(own_columns(place_window), stations_ref[...].T)
    for c in range(3):
        direction_ref[c] = offsets[c] / (WAVE_SPEED * distance)


def final_kernel(
    kept_ref,
    got_ref,
    last_ref,
    sums_ref,
    direction_ref,
    home_lag_ref,
    lag_ref,
    grad_ref,
    lag_window,
    sem,
):
    events = grad_ref.shape[1]
    stations = sums_ref.shape[0]
    part = events // 2
    span = K_REGION * part
    core = lax.axis_index("region") % 2
    sums = sums_ref[...]
    block = pl.ds(pl.multiple_of(core * stations, stations), stations)
    kept, got = kept_ref[block], got_ref[block]
    rows = []
    for h in range(2):
        values = jnp.where(core == h, kept, got)
        sums = sums + values[:, 1, span - LANES :]
        turned = jnp.concatenate([values[:, 0, :], values[:, 1, : span - LANES]], axis=1).T
        rows.append(
            jnp.concatenate([turned[n * part : (n + 1) * part] for n in range(K_REGION)], axis=1)
        )
    rows = jnp.concatenate(rows, axis=0)
    lag_window[...] = jnp.concatenate([rows, last_ref[:, rows.shape[1] :]], axis=1)
    columns = pl.ds(K_LOCAL * stations, LANES)
    lags = pltpu.make_async_copy(lag_window, lag_ref.at[:, columns], sem)
    lags.start()
    for c in range(3):
        grad_ref[c : c + 1, :] = jnp.sum(direction_ref[c] * sums, axis=0, keepdims=True)
    grad_ref[3:4, :] = jnp.sum(sums, axis=0, keepdims=True)
    lags.wait()


def params(mebibytes):
    return pltpu.CompilerParams(vmem_limit_bytes=mebibytes * 1024 * 1024)


def vmem(count):
    return [pl.BlockSpec(memory_space=pltpu.VMEM)] * count


def smem(count):
    return [pl.BlockSpec(memory_space=pltpu.SMEM)] * count


def anywhere(count):
    return [pl.BlockSpec(memory_space=pl.ANY)] * count


def shape(dims, dtype=F32):
    return jax.ShapeDtypeStruct(dims, dtype)


def other_core(block):
    count = lax.axis_size("region")
    return lax.ppermute(block, "region", [(i, i + 1 - 2 * (i % 2)) for i in range(count)])


def other_chip(block):
    odd = range(1, lax.axis_size("region") - 1, 2)
    return lax.ppermute(block, "region", [p for i in odd for p in ((i, i + 1), (i + 1, i))])


def per_device(waveforms, neighbours, masks, locations, stations):
    events, channels, samples = waveforms.shape
    neighbour_count = neighbours.shape[1]
    station_count = stations.shape[1]
    slab_count = lax.axis_size("slab")
    region_events = slab_count * events
    core = lax.axis_index("region") % 2
    part = events // 2
    span = K_REGION * part
    inverse = jnp.asarray(inverse_rows(samples))
    values = jnp.asarray(lag_values(samples))
    wave_rows = waveforms.reshape(-1, samples)
    table = jnp.asarray(forward_table(samples))
    id_columns = neighbours.T
    by_event_shape = (events, COMPONENTS + 1, station_count, samples)
    payload_rows = COMPONENTS * part + 8

    kept, sent, by_event = pl.pallas_call(
        payload_kernel,
        out_shape=(
            shape((slab_count, payload_rows, samples), BF16),
            shape((station_count, payload_rows, samples), BF16),
            shape(by_event_shape, BF16),
        ),
        in_specs=vmem(3),
        out_specs=vmem(3),
        scratch_shapes=[pltpu.VMEM((events * channels, samples), F32)],
        compiler_params=params(60),
        name="payload",
    )(wave_rows, table, id_columns)
    payload = lax.dynamic_update_slice_in_dim(
        kept, other_core(sent), (1 - core) * station_count, 0
    )
    mine = lax.all_to_all(payload, "slab", 0, 0, tiled=True)

    core_spec = other_core(by_event)
    x_spec = other_chip(by_event)

    width = K_HOME * station_count
    lag_home, sums, to_core, to_x, done = pl.pallas_call(
        home_kernel,
        out_shape=(
            shape((events, width)),
            shape((station_count, events)),
            shape((station_count, events)),
            shape((station_count, events)),
            shape((1, 1, LANES), BF16),
        ),
        in_specs=smem(1) + vmem(4) + anywhere(5),
        out_specs=vmem(5),
        scratch_shapes=[
            pltpu.VMEM((3 * events, *by_event_shape[1:]), BF16),
            pltpu.VMEM((3 * events, *by_event_shape[1:]), F32),
            pltpu.VMEM((2, BATCH * width, COMPONENTS * samples), BF16),
            pltpu.VMEM((3 * events, K_HOME * events), BF16),
            pltpu.VMEM((3, 4, LANES), F32),
            pltpu.VMEM((3, station_count, LANES), jnp.int32),
            pltpu.SemaphoreType.DMA((9,)),
        ],
        compiler_params=params(26),
        cost_estimate=pl.CostEstimate(flops=10**10, bytes_accessed=10**7, transcendentals=10**7),
        name="home",
    )(
        id_columns,
        id_columns,
        stations,
        inverse,
        values,
        core_spec,
        by_event,
        x_spec,
        locations,
        masks,
    )
    from_core = other_core(to_core)
    from_x = other_chip(to_x)
    mine = lax.dynamic_update_slice(mine, done, (0, payload_rows - 1, 0))
    other = other_core(mine)

    results = pl.pallas_call(
        task_kernel,
        out_shape=shape((slab_count, 2, LANES)),
        in_specs=smem(1) + vmem(4) + anywhere(2),
        out_specs=vmem(1)[0],
        scratch_shapes=[
            pltpu.VMEM((region_events * 8, LANES), F32),
            pltpu.VMEM((2 * span * 4, LANES), F32),
            pltpu.VMEM((2 * span * 4, LANES), F32),
            pltpu.VMEM((2 * span, COMPONENTS * samples), BF16),
            pltpu.VMEM((2 * span, COMPONENTS * samples), BF16),
            pltpu.VMEM((2 * slab_count, LANES), jnp.int32),
            pltpu.VMEM((slab_count // 2, 2 * span), F32),
            pltpu.VMEM((slab_count, 2 * span), F32),
            pltpu.VMEM((4, region_events), F32),
            pltpu.VMEM((station_count, region_events), jnp.int32),
            pltpu.SMEM((2 * slab_count, LANES), jnp.int32),
            pltpu.SemaphoreType.DMA((3,)),
        ],
        compiler_params=params(26),
        cost_estimate=pl.CostEstimate(flops=10**10, bytes_accessed=10**7, transcendentals=10**7),
        name="task",
    )(stations, mine, other, inverse, values, locations, masks)
    back = lax.all_to_all(results, "slab", 0, 0, tiled=True)
    lag_home, last, sums, direction = pl.pallas_call(
        gather_kernel,
        out_shape=(
            shape((events, neighbour_count * station_count)),
            shape((events, LANES)),
            shape((station_count, events)),
            shape((3, station_count, events)),
        ),
        in_specs=vmem(5) + anywhere(2),
        out_specs=vmem(4),
        scratch_shapes=[pltpu.VMEM((4, LANES), F32), pltpu.SemaphoreType.DMA],
        compiler_params=params(8),
        cost_estimate=pl.CostEstimate(flops=10**9, bytes_accessed=10**7, transcendentals=0),
        name="gather",
    )(lag_home, sums, from_core, from_x, stations, locations, results)
    return pl.pallas_call(
        final_kernel,
        out_shape=(
            shape((events, neighbour_count * station_count)),
            shape((4, events)),
        ),
        in_specs=vmem(5) + anywhere(1),
        out_specs=(anywhere(1)[0], vmem(1)[0]),
        scratch_shapes=[pltpu.VMEM((events, LANES), F32), pltpu.SemaphoreType.DMA],
        input_output_aliases={5: 0},
        compiler_params=params(8),
        name="final",
    )(back, other_core(back), last, sums, direction, lag_home)


def solution(mesh):
    in_specs = (P(("region", "slab"), None, None), P(("region", "slab"), None), P(), P(), P())
    out_specs = (P(("region", "slab"), None), P(None, ("region", "slab")))
    return jax.shard_map(
        per_device, mesh=mesh, in_specs=in_specs, out_specs=out_specs, check_vma=False
    )
```

```python
import functools

import jax
import jax.numpy as jnp
import ml_dtypes
import numpy as np
from jax import lax
from jax.experimental import pallas as pl
from jax.experimental.pallas import tpu as pltpu
from jax.sharding import PartitionSpec as P

K_LOCAL = 24
K_REGION = 6
K_CROSS = 2
K_HOME = K_LOCAL + K_CROSS
COMPONENTS = 3
BATCH = 4
LANES = 128

SHARPNESS = 0.1
WAVE_SPEED = 0.6
EXPONENT_SCALE = SHARPNESS * 1.4426950408889634

F32 = jnp.float32
BF16 = jnp.bfloat16
BY_LAST = (((1,), (1,)), ((), ()))


def forward_table(samples):
    half_length = samples // 2
    sample_ids = np.arange(samples)[:, None]
    cos_bins = np.arange(half_length + 1)[None, :]
    sin_bins = np.arange(1, half_length)[None, :]
    cos_angle = 2.0 * np.pi / samples * (sample_ids * cos_bins % samples)
    sin_angle = 2.0 * np.pi / samples * (sample_ids * sin_bins % samples)
    table = np.concatenate([np.cos(cos_angle), -np.sin(sin_angle)], axis=1)
    return table.astype(np.float32).astype(ml_dtypes.bfloat16)


def inverse_table(samples):
    half_length = samples // 2
    cos_bins = np.arange(half_length + 1)[:, None]
    sin_bins = np.arange(1, half_length)[:, None]
    lag_ids = np.arange(samples)[None, :]
    factors = np.where((cos_bins == 0) | (cos_bins == half_length), 1.0, 2.0) / samples
    cos_angle = 2.0 * np.pi / samples * (cos_bins * lag_ids % samples)
    sin_angle = 2.0 * np.pi / samples * (sin_bins * lag_ids % samples)
    table = np.concatenate(
        [factors * np.cos(cos_angle), -(2.0 / samples) * np.sin(sin_angle)], axis=0
    )
    return table.astype(np.float32).astype(ml_dtypes.bfloat16)


def inverse_rows(samples):
    table = inverse_table(samples)
    real, imag = table[: samples // 2], table[samples // 2 :]
    return np.concatenate([real, real, imag, imag, table], axis=0)


def lag_values(samples):
    lag_ids = np.arange(samples)
    values = np.where(lag_ids < samples // 2, lag_ids, lag_ids - samples)
    return np.broadcast_to(values[:, None], (samples, LANES)).astype(np.float32)


def arrange(first, second):
    half = first.shape[-1] // 2
    lane = lax.broadcasted_iota(jnp.int32, first.shape, first.ndim - 1)
    real = jnp.where(lane < half, first, pltpu.roll(second, half, second.ndim - 1))
    imag = jnp.where(lane < half, pltpu.roll(first, half, first.ndim - 1), second)
    return real, imag


def swapped(spec):
    return pltpu.roll(spec, spec.shape[-1] // 2, spec.ndim - 1)


def multipliers(real, imag, packed):
    half = packed.shape[-1] // 2
    lane = lax.broadcasted_iota(jnp.int32, packed.shape, packed.ndim - 1)
    edge = (lane == 0) | (lane == half)
    turned = swapped(packed)
    packed_real = jnp.where(lane <= half, packed, turned)
    packed_imag = jnp.where(edge, 0.0, jnp.where(lane < half, turned, -packed))
    return real, jnp.where(edge, imag, real), jnp.where(edge, 0.0, imag), packed_real, packed_imag


def cross(own, partner):
    real, real_edge, imag, packed_real, packed_imag = own
    other_real, other_imag, other, other_swapped = partner
    return (
        real * other_real + imag * other_imag,
        real_edge * other_imag - imag * other_real,
        packed_real * other + packed_imag * other_swapped,
    )


def soft_lags(corr, values):
    corr = corr.T
    top = jnp.max(corr, axis=0, keepdims=True)
    weights = jnp.exp2((corr - top) * EXPONENT_SCALE)
    total = jnp.sum(weights, axis=0, keepdims=True)
    moment = jnp.sum(weights * values, axis=0, keepdims=True)
    return moment / total


def all_soft_lags(crossed_ref, inverse_ref, values_ref, block):
    inverse, values = inverse_ref[...], values_ref[...]
    lags = []
    for start in range(0, crossed_ref.shape[0], block):
        corr = jnp.dot(
            crossed_ref[start : start + block, :], inverse, preferred_element_type=F32
        )
        for k in range(0, block, LANES):
            lags.append(soft_lags(corr[k : k + LANES], values))
    return jnp.concatenate(lags, axis=1)


def two_parts(x):
    high = x.astype(BF16)
    return high, (x - high.astype(F32)).astype(BF16)


def transform(wave_ref, table_ref, scr):
    block = 384

    def step(k, carry):
        rows = pl.ds(pl.multiple_of(k * block, block), block)
        spec = jnp.dot(wave_ref[rows, :], table_ref[...], preferred_element_type=F32)
        scr[rows, :] = spec.astype(BF16).astype(F32)
        return carry

    lax.fori_loop(0, wave_ref.shape[0] // block, step, 0, unroll=True)


def near_columns(ref, window, sem, region):
    slab = lax.axis_index("slab")
    start = region * (lax.axis_size("slab") * LANES // 2) + slab // 2 * LANES
    copy = pltpu.make_async_copy(
        ref.at[:, pl.ds(pl.multiple_of(start, LANES), LANES)], window, sem
    )
    copy.start()
    return copy


def own_columns(window):
    odd = lax.axis_index("slab") % 2 == 1
    values = window[...].astype(F32)
    half = values.shape[1] // 2
    return jnp.where(odd, pltpu.roll(values, half, 1), values)[:, :half]


def travel(places, station_columns):
    offsets = [places[c : c + 1, :] - station_columns[:, c : c + 1] for c in range(3)]
    return offsets, jnp.sqrt(sum(offset * offset for offset in offsets))


def three_parts(x):
    high = x.astype(BF16)
    rest = x - high.astype(F32)
    middle = rest.astype(BF16)
    return high, middle, (rest - middle.astype(F32)).astype(BF16)


def put_crossed(crossed, rows, own, partner):
    for k, values in enumerate(cross(own, partner)):
        crossed[rows, k * LANES : (k + 1) * LANES] = values.astype(BF16)


def look_up(arrival, mask, hits):
    stations = arrival.shape[0]
    rows = jnp.concatenate([p.astype(F32) for p in three_parts(arrival)] + [mask], axis=0)
    rows = jnp.dot(rows.astype(BF16), hits, preferred_element_type=F32)
    high, middle, low, found = (rows[k * stations : (k + 1) * stations] for k in range(4))
    return high + middle + low, found


def sum_by_name(residual, hits):
    stations = residual.shape[0]
    parts = jnp.concatenate(two_parts(residual), axis=0)
    sums = lax.dot_general(parts, hits, BY_LAST, preferred_element_type=F32)
    return sums[:stations] + sums[stations:]


def by_pair(lags, columns):
    turned = lags.T
    stations = turned.shape[0] // columns
    return jnp.concatenate(
        [turned[n * stations : (n + 1) * stations] for n in range(columns)], axis=1
    )


def payload_kernel(wave_ref, table_ref, ids_ref, kept_ref, sent_ref, by_event_ref, scr):
    stations = sent_ref.shape[0]
    events = ids_ref.shape[1]
    part = events // 2
    channels = stations * COMPONENTS
    core = lax.axis_index("region") % 2
    transform(wave_ref, table_ref, scr)
    ids = ids_ref[K_LOCAL : K_LOCAL + K_REGION, :]
    tail = sent_ref.shape[1] - COMPONENTS * part
    for out, base, half in ((kept_ref, core * stations, core), (sent_ref, 0, 1 - core)):
        mine = jnp.where(half == 1, ids[:, part:], ids[:, :part])
        row = jnp.concatenate([mine[n : n + 1] for n in range(K_REGION)], axis=1)
        row = jnp.concatenate([row, jnp.zeros((1, 2 * LANES - row.shape[1]), jnp.int32)], axis=1)
        source, event = row // events % (2 * stations), row % events
        rows = jnp.concatenate(
            [source[:, :LANES], source[:, LANES:], event[:, :LANES], event[:, LANES:]]
            + [jnp.zeros((tail - 4, LANES), jnp.int32)],
            axis=0,
        )
        rows = rows.astype(F32).astype(BF16)
        for s in range(stations):
            first, second, third = (
                scr[pl.ds(half * (part * channels) + COMPONENTS * s + c, part, stride=channels), :]
                for c in range(COMPONENTS)
            )
            for k, values in enumerate((*arrange(first, second), third)):
                out[base + s, k * part : (k + 1) * part, :] = values.astype(BF16)
            out[base + s, COMPONENTS * part :, :] = rows

    def one_event(event, carry):
        first, second, third = (
            scr[pl.ds(event * channels + c, stations, stride=COMPONENTS), :]
            for c in range(COMPONENTS)
        )
        for k, values in enumerate((*arrange(first, second), third, swapped(third))):
            by_event_ref[event, k] = values.astype(BF16)
        return carry

    lax.fori_loop(0, events, one_event, 0, unroll=8)


def home_kernel(
    ids,
    id_ref,
    stations_ref,
    inverse_ref,
    values_ref,
    core_ref,
    own_ref,
    x_ref,
    locations_ref,
    masks_ref,
    lag_ref,
    sums_ref,
    to_core_ref,
    to_x_ref,
    done_ref,
    raw,
    pool,
    crossed,
    hits,
    place_windows,
    mask_windows,
    sems,
):
    events, _, stations, _ = own_ref.shape
    width = K_HOME * stations
    batches = events // BATCH
    region = lax.axis_index("region")
    last = lax.axis_size("region") - 1
    copies = [
        pltpu.make_async_copy(ref, raw.at[pl.ds(k * events, events)], sems.at[k])
        for k, ref in enumerate((core_ref, own_ref, x_ref))
    ]
    for copy in copies:
        copy.start()
    odd = region % 2
    near = (region + 1 - 2 * odd, region, jnp.clip(region - 1 + 2 * odd, 0, last))
    for k, where in enumerate(near):
        copies.append(near_columns(locations_ref, place_windows.at[k], sems.at[3 + k], where))
        copies.append(near_columns(masks_ref, mask_windows.at[k], sems.at[6 + k], where))
    blocks = [events] * K_LOCAL + [
        jnp.where((odd == 1) | (region == 0), 0, 2 * events),
        jnp.where((odd == 0) | (region == last), 0, 2 * events),
    ]
    columns = [*range(K_LOCAL), *range(K_LOCAL + K_REGION, K_LOCAL + K_REGION + K_CROSS)]
    named = lax.broadcasted_iota(jnp.int32, (3 * events, events), 0)
    for n in range(0, K_HOME, 2):
        pair = [
            jnp.where(
                id_ref[columns[m] : columns[m] + 1, :] % events + blocks[m] == named, 1.0, 0.0
            )
            for m in (n, n + 1)
        ]
        hits[:, n * events : (n + 2) * events] = jnp.concatenate(pair, axis=1).astype(BF16)
    done_ref[...] = jnp.zeros(done_ref.shape, done_ref.dtype)
    for copy in copies:
        copy.wait()

    def widen(event, carry):
        pool[event] = raw[event].astype(F32)
        return carry

    lax.fori_loop(0, 3 * events, widen, 0, unroll=8)

    def cross_batch(batch, rows_ref):
        for b in range(BATCH):
            event = batch * BATCH + b
            own = multipliers(*(pool[events + event, k] for k in range(COMPONENTS)))
            for n in range(K_HOME):
                j = lax.bitwise_and(ids[columns[n], event], events - 1) + blocks[n]
                partner = [pool[j, k] for k in range(COMPONENTS + 1)]
                start = b * width + n * stations
                put_crossed(rows_ref, slice(start, start + stations), own, partner)

    def finish_batch(batch, rows_ref):
        lags = all_soft_lags(rows_ref, inverse_ref, values_ref, BATCH * width)
        for b in range(BATCH):
            lag_ref[pl.ds(batch * BATCH + b, 1), :] = lags[:, b * width : (b + 1) * width]

    def two_batches(step, carry):
        cross_batch(2 * step + 1, crossed.at[1])
        finish_batch(2 * step, crossed.at[0])
        cross_batch(jnp.minimum(2 * step + 2, batches - 1), crossed.at[0])
        finish_batch(2 * step + 1, crossed.at[1])
        return carry

    cross_batch(0, crossed.at[0])
    lax.fori_loop(0, batches // 2, two_batches, 0)

    station_columns = stations_ref[...].T
    arrivals, masks = [], []
    for k in range(3):
        places = own_columns(place_windows.at[k])
        masks.append(own_columns(mask_windows.at[k]))
        _, distance = travel(places, station_columns)
        arrivals.append(places[3:4, :] + distance / WAVE_SPEED)
    near_arrivals, found = look_up(
        jnp.concatenate(arrivals, axis=1), jnp.concatenate(masks, axis=1), hits[...]
    )
    residual = (
        jnp.tile(masks[1], (1, K_HOME))
        * found
        * (by_pair(lag_ref[...], K_HOME) - (near_arrivals - jnp.tile(arrivals[1], (1, K_HOME))))
        * (1.0 / ((K_HOME + K_REGION) * stations))
    )
    own_sums = sum(residual[:, n * events : (n + 1) * events] for n in range(K_HOME))
    sums = sum_by_name(residual, hits[...])
    to_core_ref[...] = sums[:, :events]
    sums_ref[...] = own_sums - sums[:, events : 2 * events]
    to_x_ref[...] = sums[:, 2 * events :]


def pair_ids(id_rows, step, span):
    pieces = []
    for u in range(2):
        row = 4 * step + 2 * u
        pieces.append(id_rows[pl.ds(row, 1), :])
        pieces.append(id_rows[pl.ds(row + 1, 1), :][:, : span - LANES])
    return jnp.concatenate(pieces, axis=1)


def lookup_kernel(
    stations_ref,
    mine_ref,
    locations_ref,
    masks_ref,
    id_rows,
    found_ref,
    own_terms,
    place_window,
    mask_window,
    sems,
):
    sources, payload, _ = mine_ref.shape
    stations = sources // 2
    part = payload // COMPONENTS // 8 * 8
    events = 2 * part
    span = K_REGION * part
    width = 2 * span
    region_events = sources * events
    region, slab = lax.axis_index("region"), lax.axis_index("slab")
    core = region % 2
    task_region = region - core + slab // stations
    station = slab % stations
    columns = pl.ds(pl.multiple_of(task_region * region_events, region_events), region_events)
    copies = [
        pltpu.make_async_copy(locations_ref.at[:, columns], place_window, sems.at[0]),
        pltpu.make_async_copy(masks_ref.at[:, columns], mask_window, sems.at[1]),
    ]
    for copy in copies:
        copy.start()

    def read_ids(source, carry):
        tail = mine_ref[source, COMPONENTS * part :, :].astype(F32)
        rows = ((tail[:2] * events + tail[2:4]) * 8).astype(jnp.int32)
        id_rows[pl.ds(2 * source, 1), :] = rows[:1]
        id_rows[pl.ds(2 * source + 1, 1), :] = rows[1:]
        return carry

    lax.fori_loop(0, sources, read_ids, 0, unroll=8)
    for copy in copies:
        copy.wait()
    offsets = [place_window[c : c + 1, :] - stations_ref[c, station] for c in range(3)]
    arrival = place_window[3:4, :] + (
        jnp.sqrt(sum(offset * offset for offset in offsets)) / WAVE_SPEED
    )
    mask = mask_window[pl.ds(station, 1), :].astype(F32)

    def as_rows(row):
        return jnp.concatenate(
            [row[:, t * LANES : (t + 1) * LANES] for t in range(region_events // LANES)], axis=0
        )

    tables = jnp.concatenate(
        [part_of.astype(F32) for part_of in three_parts(as_rows(arrival))] + [as_rows(mask)], axis=0
    ).astype(BF16)
    half_rows = tables.shape[0] // 4
    lane = lax.broadcasted_iota(jnp.int32, (LANES, width), 1)
    event_rows = lax.broadcasted_iota(jnp.int32, (LANES, width), 0)
    own_hits = event_rows == lane // span * events + core * part + lane % part
    own_hits = jnp.where(own_hits, 1.0, 0.0).astype(BF16)
    own = jnp.dot(tables, own_hits, preferred_element_type=F32)
    own_terms[:half_rows] = own[:half_rows] + own[half_rows : 2 * half_rows] + own[
        2 * half_rows : 3 * half_rows
    ]
    own_terms[half_rows:] = own[3 * half_rows :]
    source_rows = lax.broadcasted_iota(jnp.int32, (half_rows, width), 0)

    def two_sources(step, carry):
        id_row = pair_ids(id_rows, step, span) // 8
        from_source = source_rows == id_row // LANES
        from_event = jnp.where(event_rows == id_row % LANES, 1.0, 0.0).astype(BF16)
        looked_up = jnp.dot(tables, from_event, preferred_element_type=F32)
        arrival = looked_up[:half_rows] + looked_up[half_rows : 2 * half_rows]
        arrival = arrival + looked_up[2 * half_rows : 3 * half_rows]
        mask = jnp.where(from_source, looked_up[3 * half_rows :], 0.0)
        found_ref[pl.ds(step, 1), :] = jnp.sum(
            jnp.where(from_source, arrival, 0.0), axis=0, keepdims=True
        )
        found_ref[pl.ds(half_rows + step, 1), :] = jnp.sum(mask, axis=0, keepdims=True)
        return carry

    lax.fori_loop(0, half_rows, two_sources, 0, unroll=4)


def task_kernel(
    id_rows,
    found_ref,
    own_terms,
    mine_ref,
    other_ref,
    inverse_ref,
    values_ref,
    out_ref,
    table,
    fetched_even,
    fetched_odd,
    crossed_even,
    crossed_odd,
    residuals,
    ids,
    sem,
):
    sources, payload, _ = mine_ref.shape
    stations = sources // 2
    part = payload // COMPONENTS // 8 * 8
    events = 2 * part
    span = K_REGION * part
    width = 2 * span
    core = lax.axis_index("region") % 2
    half_rows = sources // 2
    id_copy = pltpu.make_async_copy(id_rows, ids, sem)
    id_copy.start()

    def fill(source, carry):
        for ref, half in ((mine_ref, core), (other_ref, 1 - core)):
            rows = [
                ref[source, k * part : (k + 1) * part, :].astype(F32) for k in range(COMPONENTS)
            ]
            rows.append(swapped(rows[-1]))
            base = (source * events + half * part) * 8
            for k, values_k in enumerate(rows):
                table[pl.ds(base + k, part, stride=8), :] = values_k
                table[pl.ds(base + 4 + k, part, stride=8), :] = values_k
        return carry

    lax.fori_loop(0, sources, fill, 0, unroll=4)
    id_copy.wait()
    lane = lax.broadcasted_iota(jnp.int32, (LANES, width), 1)
    event_rows = lax.broadcasted_iota(jnp.int32, (LANES, width), 0)
    own_hits = event_rows == lane // span * events + core * part + lane % part
    own_hits = jnp.where(own_hits, 1.0, 0.0).astype(BF16)

    upper = lax.broadcasted_iota(jnp.int32, (8, LANES), 0) < 4
    source_rows = lax.broadcasted_iota(jnp.int32, (half_rows, width), 0)
    out_lane = lax.broadcasted_iota(jnp.int32, (1, LANES), 1)

    def fetch(step, into):
        for q in range(0, width, 2):
            row, column = q // span * 2 + q % span // LANES, q % span % LANES
            first = ids[step * 4 + row, column]
            second = ids[step * 4 + row, column + 1]
            first = table[pl.ds(pl.multiple_of(first, 8), 8), :]
            second = table[pl.ds(pl.multiple_of(second, 8), 8), :]
            into[q * 4 : q * 4 + 8, :] = jnp.where(upper, first, second)

    def cross_two(step, source, into):
        for u in range(2):
            own = multipliers(
                *(
                    mine_ref[2 * step + u, k * part : (k + 1) * part, :].astype(F32)
                    for k in range(COMPONENTS)
                )
            )
            for n in range(K_REGION):
                start = u * span + n * part
                partner = [
                    source[pl.ds(start * 4 + k, part, stride=4), :]
                    for k in range(COMPONENTS + 1)
                ]
                put_crossed(into, slice(start, start + part), own, partner)

    def finish(step, rows_ref, sums):
        lag = all_soft_lags(rows_ref, inverse_ref, values_ref, LANES)
        for u in range(2):
            rest = lag[:, u * span + LANES : (u + 1) * span]
            rest = jnp.concatenate([rest, jnp.zeros((1, LANES - rest.shape[1]), F32)], axis=1)
            out_ref[2 * step + u] = jnp.concatenate(
                [lag[:, u * span : u * span + LANES], rest], axis=0
            )
        id_row = pair_ids(id_rows, step, span) // 8
        from_source = source_rows == id_row // LANES
        from_event = jnp.where(event_rows == id_row % LANES, 1.0, 0.0).astype(BF16)
        arrival = found_ref[pl.ds(step, 1), :]
        mask = found_ref[pl.ds(half_rows + step, 1), :]
        residual = (
            own_terms[pl.ds(half_rows + step, 1), :]
            * mask
            * (lag - (arrival - own_terms[pl.ds(step, 1), :]))
            * (1.0 / ((K_LOCAL + K_REGION + K_CROSS) * stations))
        )
        residuals[pl.ds(step, 1), :] = residual
        terms = jnp.concatenate(two_parts(jnp.where(from_source, residual, 0.0)), axis=0)
        return sums + lax.dot_general(terms, from_event, BY_LAST, preferred_element_type=F32)

    steps = sources // 2

    def two_steps(pair, sums):
        first = 2 * pair
        fetch(jnp.minimum(first + 2, steps - 1), fetched_even)
        cross_two(first + 1, fetched_odd, crossed_odd)
        sums = finish(first, crossed_even, sums)
        fetch(jnp.minimum(first + 3, steps - 1), fetched_odd)
        cross_two(jnp.minimum(first + 2, steps - 1), fetched_even, crossed_even)
        return finish(first + 1, crossed_odd, sums)

    fetch(0, fetched_even)
    cross_two(0, fetched_even, crossed_even)
    fetch(1, fetched_odd)
    sums = lax.fori_loop(0, steps // 2, two_steps, jnp.zeros((2 * half_rows, LANES), F32))
    terms = jnp.concatenate(two_parts(residuals[...]), axis=0)
    sums = lax.dot_general(terms, own_hits, BY_LAST, preferred_element_type=F32) - sums
    sums = sums[:half_rows] + sums[half_rows:]
    for t in range(half_rows):
        for u in range(2):
            row = sums[t : t + 1, :]
            row = pltpu.roll(row, LANES // 2, 1) if u == 0 else row
            lags = out_ref[2 * t + u]
            out_ref[2 * t + u] = jnp.concatenate(
                [lags[:1], jnp.where(out_lane < span - LANES, lags[1:], row)], axis=0
            )


def gather_kernel(
    home_lag_ref,
    sums_ref,
    core_ref,
    x_ref,
    stations_ref,
    locations_ref,
    order_ref,
    lag_ref,
    last_ref,
    out_ref,
    direction_ref,
    place_window,
    sem,
):
    stations, events = sums_ref.shape
    copy = near_columns(locations_ref, place_window, sem, lax.axis_index("region"))
    local = K_LOCAL * stations
    remote = K_REGION * stations
    home = home_lag_ref[...]
    gap = jnp.zeros((events, remote), F32)
    last = jnp.concatenate([gap, home[:, local:]], axis=1)
    last_ref[...] = last
    lag_ref[...] = jnp.concatenate([home[:, :local], last], axis=1)
    out_ref[...] = sums_ref[...] - core_ref[...] - x_ref[...]
    copy.wait()
    offsets, distance = travel(own_columns(place_window), stations_ref[...].T)
    for c in range(3):
        direction_ref[c] = offsets[c] / (WAVE_SPEED * distance)


def final_kernel(
    kept_ref,
    got_ref,
    last_ref,
    sums_ref,
    direction_ref,
    home_lag_ref,
    lag_ref,
    grad_ref,
    lag_window,
    sem,
):
    events = grad_ref.shape[1]
    stations = sums_ref.shape[0]
    part = events // 2
    span = K_REGION * part
    core = lax.axis_index("region") % 2
    sums = sums_ref[...]
    block = pl.ds(pl.multiple_of(core * stations, stations), stations)
    kept, got = kept_ref[block], got_ref[block]
    rows = []
    for h in range(2):
        values = jnp.where(core == h, kept, got)
        sums = sums + values[:, 1, span - LANES :]
        turned = jnp.concatenate([values[:, 0, :], values[:, 1, : span - LANES]], axis=1).T
        rows.append(
            jnp.concatenate([turned[n * part : (n + 1) * part] for n in range(K_REGION)], axis=1)
        )
    rows = jnp.concatenate(rows, axis=0)
    lag_window[...] = jnp.concatenate([rows, last_ref[:, rows.shape[1] :]], axis=1)
    columns = pl.ds(K_LOCAL * stations, LANES)
    lags = pltpu.make_async_copy(lag_window, lag_ref.at[:, columns], sem)
    lags.start()
    for c in range(3):
        grad_ref[c : c + 1, :] = jnp.sum(direction_ref[c] * sums, axis=0, keepdims=True)
    grad_ref[3:4, :] = jnp.sum(sums, axis=0, keepdims=True)
    lags.wait()


def params(mebibytes):
    return pltpu.CompilerParams(vmem_limit_bytes=mebibytes * 1024 * 1024)


def vmem(count):
    return [pl.BlockSpec(memory_space=pltpu.VMEM)] * count


def smem(count):
    return [pl.BlockSpec(memory_space=pltpu.SMEM)] * count


def anywhere(count):
    return [pl.BlockSpec(memory_space=pl.ANY)] * count


def shape(dims, dtype=F32):
    return jax.ShapeDtypeStruct(dims, dtype)


def other_core(block):
    count = lax.axis_size("region")
    return lax.ppermute(block, "region", [(i, i + 1 - 2 * (i % 2)) for i in range(count)])


def other_chip(block):
    odd = range(1, lax.axis_size("region") - 1, 2)
    return lax.ppermute(block, "region", [p for i in odd for p in ((i, i + 1), (i + 1, i))])


def per_device(waveforms, neighbours, masks, locations, stations):
    events, channels, samples = waveforms.shape
    neighbour_count = neighbours.shape[1]
    station_count = stations.shape[1]
    slab_count = lax.axis_size("slab")
    region_events = slab_count * events
    core = lax.axis_index("region") % 2
    part = events // 2
    span = K_REGION * part
    inverse = jnp.asarray(inverse_rows(samples))
    values = jnp.asarray(lag_values(samples))
    wave_rows = waveforms.reshape(-1, samples)
    table = jnp.asarray(forward_table(samples))
    id_columns = neighbours.T
    by_event_shape = (events, COMPONENTS + 1, station_count, samples)
    payload_rows = COMPONENTS * part + 8

    kept, sent, by_event = pl.pallas_call(
        payload_kernel,
        out_shape=(
            shape((slab_count, payload_rows, samples), BF16),
            shape((station_count, payload_rows, samples), BF16),
            shape(by_event_shape, BF16),
        ),
        in_specs=vmem(3),
        out_specs=vmem(3),
        scratch_shapes=[pltpu.VMEM((events * channels, samples), F32)],
        compiler_params=params(60),
        name="payload",
    )(wave_rows, table, id_columns)
    payload = lax.dynamic_update_slice_in_dim(
        kept, other_core(sent), (1 - core) * station_count, 0
    )
    mine = lax.all_to_all(payload, "slab", 0, 0, tiled=True)

    core_spec = other_core(by_event)
    x_spec = other_chip(by_event)

    width = K_HOME * station_count
    lag_home, sums, to_core, to_x, done = pl.pallas_call(
        home_kernel,
        out_shape=(
            shape((events, width)),
            shape((station_count, events)),
            shape((station_count, events)),
            shape((station_count, events)),
            shape((1, 1, LANES), BF16),
        ),
        in_specs=smem(1) + vmem(4) + anywhere(5),
        out_specs=vmem(5),
        scratch_shapes=[
            pltpu.VMEM((3 * events, *by_event_shape[1:]), BF16),
            pltpu.VMEM((3 * events, *by_event_shape[1:]), F32),
            pltpu.VMEM((2, BATCH * width, COMPONENTS * samples), BF16),
            pltpu.VMEM((3 * events, K_HOME * events), BF16),
            pltpu.VMEM((3, 4, LANES), F32),
            pltpu.VMEM((3, station_count, LANES), jnp.int32),
            pltpu.SemaphoreType.DMA((9,)),
        ],
        compiler_params=params(26),
        cost_estimate=pl.CostEstimate(flops=10**10, bytes_accessed=10**7, transcendentals=10**7),
        name="home",
    )(
        id_columns,
        id_columns,
        stations,
        inverse,
        values,
        core_spec,
        by_event,
        x_spec,
        locations,
        masks,
    )
    from_core = other_core(to_core)
    from_x = other_chip(to_x)
    mine = lax.dynamic_update_slice(mine, done, (0, payload_rows - 1, 0))
    other = other_core(mine)

    id_rows, found, own_terms = pl.pallas_call(
        lookup_kernel,
        out_shape=(
            shape((2 * slab_count, LANES), jnp.int32),
            shape((slab_count, 2 * span)),
            shape((slab_count, 2 * span)),
        ),
        in_specs=smem(1) + vmem(1) + anywhere(2),
        out_specs=vmem(3),
        scratch_shapes=[
            pltpu.VMEM((4, region_events), F32),
            pltpu.VMEM((station_count, region_events), jnp.int32),
            pltpu.SemaphoreType.DMA((2,)),
        ],
        compiler_params=params(16),
        cost_estimate=pl.CostEstimate(flops=10**9, bytes_accessed=10**7, transcendentals=0),
        name="lookup",
    )(stations, mine, locations, masks)
    results = pl.pallas_call(
        task_kernel,
        out_shape=shape((slab_count, 2, LANES)),
        in_specs=vmem(7),
        out_specs=vmem(1)[0],
        scratch_shapes=[
            pltpu.VMEM((region_events * 8, LANES), F32),
            pltpu.VMEM((2 * span * 4, LANES), F32),
            pltpu.VMEM((2 * span * 4, LANES), F32),
            pltpu.VMEM((2 * span, COMPONENTS * samples), BF16),
            pltpu.VMEM((2 * span, COMPONENTS * samples), BF16),
            pltpu.VMEM((slab_count // 2, 2 * span), F32),
            pltpu.SMEM((2 * slab_count, LANES), jnp.int32),
            pltpu.SemaphoreType.DMA,
        ],
        compiler_params=params(26),
        cost_estimate=pl.CostEstimate(flops=10**10, bytes_accessed=10**7, transcendentals=10**7),
        name="task",
    )(id_rows, found, own_terms, mine, other, inverse, values)
    back = lax.all_to_all(results, "slab", 0, 0, tiled=True)
    lag_home, last, sums, direction = pl.pallas_call(
        gather_kernel,
        out_shape=(
            shape((events, neighbour_count * station_count)),
            shape((events, LANES)),
            shape((station_count, events)),
            shape((3, station_count, events)),
        ),
        in_specs=vmem(5) + anywhere(2),
        out_specs=vmem(4),
        scratch_shapes=[pltpu.VMEM((4, LANES), F32), pltpu.SemaphoreType.DMA],
        compiler_params=params(8),
        cost_estimate=pl.CostEstimate(flops=10**9, bytes_accessed=10**7, transcendentals=0),
        name="gather",
    )(lag_home, sums, from_core, from_x, stations, locations, results)
    return pl.pallas_call(
        final_kernel,
        out_shape=(
            shape((events, neighbour_count * station_count)),
            shape((4, events)),
        ),
        in_specs=vmem(5) + anywhere(1),
        out_specs=(anywhere(1)[0], vmem(1)[0]),
        scratch_shapes=[pltpu.VMEM((events, LANES), F32), pltpu.SemaphoreType.DMA],
        input_output_aliases={5: 0},
        compiler_params=params(8),
        name="final",
    )(back, other_core(back), last, sums, direction, lag_home)


def solution(mesh):
    in_specs = (P(("region", "slab"), None, None), P(("region", "slab"), None), P(), P(), P())
    out_specs = (P(("region", "slab"), None), P(None, ("region", "slab")))
    return jax.shard_map(
        per_device, mesh=mesh, in_specs=in_specs, out_specs=out_specs, check_vma=False
    )
```

```python
import functools

import jax
import jax.numpy as jnp
import ml_dtypes
import numpy as np
from jax import lax
from jax.experimental import pallas as pl
from jax.experimental.pallas import tpu as pltpu
from jax.sharding import PartitionSpec as P

K_LOCAL = 24
K_REGION = 6
K_CROSS = 2
K_HOME = K_LOCAL + K_CROSS
COMPONENTS = 3
BATCH = 4
LANES = 128

SHARPNESS = 0.1
WAVE_SPEED = 0.6
EXPONENT_SCALE = SHARPNESS * 1.4426950408889634

F32 = jnp.float32
BF16 = jnp.bfloat16
BY_LAST = (((1,), (1,)), ((), ()))


def forward_table(samples):
    half_length = samples // 2
    sample_ids = np.arange(samples)[:, None]
    cos_bins = np.arange(half_length + 1)[None, :]
    sin_bins = np.arange(1, half_length)[None, :]
    cos_angle = 2.0 * np.pi / samples * (sample_ids * cos_bins % samples)
    sin_angle = 2.0 * np.pi / samples * (sample_ids * sin_bins % samples)
    table = np.concatenate([np.cos(cos_angle), -np.sin(sin_angle)], axis=1)
    return table.astype(np.float32).astype(ml_dtypes.bfloat16)


def inverse_table(samples):
    half_length = samples // 2
    cos_bins = np.arange(half_length + 1)[:, None]
    sin_bins = np.arange(1, half_length)[:, None]
    lag_ids = np.arange(samples)[None, :]
    factors = np.where((cos_bins == 0) | (cos_bins == half_length), 1.0, 2.0) / samples
    cos_angle = 2.0 * np.pi / samples * (cos_bins * lag_ids % samples)
    sin_angle = 2.0 * np.pi / samples * (sin_bins * lag_ids % samples)
    table = np.concatenate(
        [factors * np.cos(cos_angle), -(2.0 / samples) * np.sin(sin_angle)], axis=0
    )
    return table.astype(np.float32).astype(ml_dtypes.bfloat16)


def inverse_rows(samples):
    table = inverse_table(samples)
    real, imag = table[: samples // 2], table[samples // 2 :]
    return np.concatenate([real, real, imag, imag, table], axis=0)


def arrange(first, second):
    half = first.shape[-1] // 2
    lane = lax.broadcasted_iota(jnp.int32, first.shape, first.ndim - 1)
    real = jnp.where(lane < half, first, pltpu.roll(second, half, second.ndim - 1))
    imag = jnp.where(lane < half, pltpu.roll(first, half, first.ndim - 1), second)
    return real, imag


def swapped(spec):
    return pltpu.roll(spec, spec.shape[-1] // 2, spec.ndim - 1)


def multipliers(real, imag, packed):
    half = packed.shape[-1] // 2
    lane = lax.broadcasted_iota(jnp.int32, packed.shape, packed.ndim - 1)
    edge = (lane == 0) | (lane == half)
    turned = swapped(packed)
    packed_real = jnp.where(lane <= half, packed, turned)
    packed_imag = jnp.where(edge, 0.0, jnp.where(lane < half, turned, -packed))
    return real, jnp.where(edge, imag, real), jnp.where(edge, 0.0, imag), packed_real, packed_imag


def cross(own, partner):
    real, real_edge, imag, packed_real, packed_imag = own
    other_real, other_imag, other, other_swapped = partner
    return (
        real * other_real + imag * other_imag,
        real_edge * other_imag - imag * other_real,
        packed_real * other + packed_imag * other_swapped,
    )


def soft_lags(corr):
    top = jnp.max(corr, axis=0, keepdims=True)
    weights = jnp.exp2((corr - top) * EXPONENT_SCALE)
    groups = [weights[k : k + 8] for k in range(0, weights.shape[0], 8)]
    half = len(groups) // 2
    after = groups[half - 1]
    ahead = after
    for k in range(half - 2, 0, -1):
        after = after + groups[k]
        ahead = ahead + after
    after = after + groups[0]
    before = groups[half]
    behind = before
    for k in range(half + 1, len(groups)):
        before = before + groups[k]
        behind = behind + before
    total = after + before
    row = lax.broadcasted_iota(jnp.int32, total.shape, 0).astype(F32)
    moment = jnp.sum((ahead - behind) * 8.0 + row * total, axis=0, keepdims=True)
    return moment / jnp.sum(total, axis=0, keepdims=True)


def all_soft_lags(crossed_ref, inverse_ref):
    corr = jnp.dot(crossed_ref[...], inverse_ref[...], preferred_element_type=F32)
    lags = [soft_lags(corr[k : k + LANES].T) for k in range(0, corr.shape[0], LANES)]
    return jnp.concatenate(lags, axis=1)


def soft_lags_by_block(crossed_ref, turned_ref):
    lags = []
    for k in range(0, crossed_ref.shape[0], LANES):
        rows = crossed_ref[k : k + LANES, :]
        corr = lax.dot_general(turned_ref[...], rows, BY_LAST, preferred_element_type=F32)
        lags.append(soft_lags(corr))
    return jnp.concatenate(lags, axis=1)


def two_parts(x):
    high = x.astype(BF16)
    return high, (x - high.astype(F32)).astype(BF16)


def transform(wave_ref, table_ref, scr):
    block = 384

    def step(k, carry):
        rows = pl.ds(pl.multiple_of(k * block, block), block)
        spec = jnp.dot(wave_ref[rows, :], table_ref[...], preferred_element_type=F32)
        scr[rows, :] = spec.astype(BF16).astype(F32)
        return carry

    lax.fori_loop(0, wave_ref.shape[0] // block, step, 0, unroll=True)


def near_columns(ref, window, sem, region):
    slab = lax.axis_index("slab")
    start = region * (lax.axis_size("slab") * LANES // 2) + slab // 2 * LANES
    copy = pltpu.make_async_copy(
        ref.at[:, pl.ds(pl.multiple_of(start, LANES), LANES)], window, sem
    )
    copy.start()
    return copy


def own_columns(window):
    odd = lax.axis_index("slab") % 2 == 1
    values = window[...].astype(F32)
    half = values.shape[1] // 2
    return jnp.where(odd, pltpu.roll(values, half, 1), values)[:, :half]


def travel(places, station_columns):
    offsets = [places[c : c + 1, :] - station_columns[:, c : c + 1] for c in range(3)]
    return offsets, jnp.sqrt(sum(offset * offset for offset in offsets))


def three_parts(x):
    high = x.astype(BF16)
    rest = x - high.astype(F32)
    middle = rest.astype(BF16)
    return high, middle, (rest - middle.astype(F32)).astype(BF16)


def put_crossed(crossed, rows, own, partner):
    for k, values in enumerate(cross(own, partner)):
        crossed[rows, k * LANES : (k + 1) * LANES] = values.astype(BF16)


def look_up(arrival, mask, hits):
    stations = arrival.shape[0]
    rows = jnp.concatenate([p.astype(F32) for p in three_parts(arrival)] + [mask], axis=0)
    rows = jnp.dot(rows.astype(BF16), hits, preferred_element_type=F32)
    high, middle, low, found = (rows[k * stations : (k + 1) * stations] for k in range(4))
    return high + middle + low, found


def sum_by_name(residual, hits):
    stations = residual.shape[0]
    parts = jnp.concatenate(two_parts(residual), axis=0)
    sums = lax.dot_general(parts, hits, BY_LAST, preferred_element_type=F32)
    return sums[:stations] + sums[stations:]


def by_pair(lags, columns):
    turned = lags.T
    stations = turned.shape[0] // columns
    return jnp.concatenate(
        [turned[n * stations : (n + 1) * stations] for n in range(columns)], axis=1
    )


def payload_kernel(wave_ref, table_ref, ids_ref, kept_ref, sent_ref, by_event_ref, scr):
    stations = sent_ref.shape[0]
    events = ids_ref.shape[1]
    part = events // 2
    channels = stations * COMPONENTS
    core = lax.axis_index("region") % 2
    transform(wave_ref, table_ref, scr)
    ids = ids_ref[K_LOCAL : K_LOCAL + K_REGION, :]
    tail = sent_ref.shape[1] - COMPONENTS * part
    for out, base, half in ((kept_ref, core * stations, core), (sent_ref, 0, 1 - core)):
        mine = jnp.where(half == 1, ids[:, part:], ids[:, :part])
        row = jnp.concatenate([mine[n : n + 1] for n in range(K_REGION)], axis=1)
        row = jnp.concatenate([row, jnp.zeros((1, 2 * LANES - row.shape[1]), jnp.int32)], axis=1)
        source, event = row // events % (2 * stations), row % events
        rows = jnp.concatenate(
            [source[:, :LANES], source[:, LANES:], event[:, :LANES], event[:, LANES:]]
            + [jnp.zeros((tail - 4, LANES), jnp.int32)],
            axis=0,
        )
        rows = rows.astype(F32).astype(BF16)
        for s in range(stations):
            first, second, third = (
                scr[pl.ds(half * (part * channels) + COMPONENTS * s + c, part, stride=channels), :]
                for c in range(COMPONENTS)
            )
            for k, values in enumerate((*arrange(first, second), third)):
                out[base + s, k * part : (k + 1) * part, :] = values.astype(BF16)
            out[base + s, COMPONENTS * part :, :] = rows

    def one_event(event, carry):
        first, second, third = (
            scr[pl.ds(event * channels + c, stations, stride=COMPONENTS), :]
            for c in range(COMPONENTS)
        )
        for k, values in enumerate((*arrange(first, second), third, swapped(third))):
            by_event_ref[event, k] = values.astype(BF16)
        return carry

    lax.fori_loop(0, events, one_event, 0, unroll=8)


def home_kernel(
    ids,
    id_ref,
    stations_ref,
    inverse_ref,
    core_ref,
    own_ref,
    x_ref,
    locations_ref,
    masks_ref,
    lag_ref,
    sums_ref,
    to_core_ref,
    to_x_ref,
    done_ref,
    raw,
    pool,
    crossed,
    hits,
    place_windows,
    mask_windows,
    sems,
):
    events, _, stations, _ = own_ref.shape
    width = K_HOME * stations
    batches = events // BATCH
    region = lax.axis_index("region")
    last = lax.axis_size("region") - 1
    copies = [
        pltpu.make_async_copy(ref, raw.at[pl.ds(k * events, events)], sems.at[k])
        for k, ref in enumerate((core_ref, own_ref, x_ref))
    ]
    for copy in copies:
        copy.start()
    odd = region % 2
    near = (region + 1 - 2 * odd, region, jnp.clip(region - 1 + 2 * odd, 0, last))
    for k, where in enumerate(near):
        copies.append(near_columns(locations_ref, place_windows.at[k], sems.at[3 + k], where))
        copies.append(near_columns(masks_ref, mask_windows.at[k], sems.at[6 + k], where))
    blocks = [events] * K_LOCAL + [
        jnp.where((odd == 1) | (region == 0), 0, 2 * events),
        jnp.where((odd == 0) | (region == last), 0, 2 * events),
    ]
    columns = [*range(K_LOCAL), *range(K_LOCAL + K_REGION, K_LOCAL + K_REGION + K_CROSS)]
    named = lax.broadcasted_iota(jnp.int32, (3 * events, events), 0)
    for n in range(0, K_HOME, 2):
        pair = [
            jnp.where(
                id_ref[columns[m] : columns[m] + 1, :] % events + blocks[m] == named, 1.0, 0.0
            )
            for m in (n, n + 1)
        ]
        hits[:, n * events : (n + 2) * events] = jnp.concatenate(pair, axis=1).astype(BF16)
    done_ref[...] = jnp.zeros(done_ref.shape, done_ref.dtype)
    for copy in copies:
        copy.wait()

    def widen(event, carry):
        pool[event] = raw[event].astype(F32)
        return carry

    lax.fori_loop(0, 3 * events, widen, 0, unroll=8)

    def cross_batch(batch, rows_ref):
        for b in range(BATCH):
            event = batch * BATCH + b
            own = multipliers(*(pool[events + event, k] for k in range(COMPONENTS)))
            for n in range(K_HOME):
                j = lax.bitwise_and(ids[columns[n], event], events - 1) + blocks[n]
                partner = [pool[j, k] for k in range(COMPONENTS + 1)]
                start = b * width + n * stations
                put_crossed(rows_ref, slice(start, start + stations), own, partner)

    def finish_batch(batch, rows_ref):
        lags = all_soft_lags(rows_ref, inverse_ref)
        for b in range(BATCH):
            lag_ref[pl.ds(batch * BATCH + b, 1), :] = lags[:, b * width : (b + 1) * width]

    def two_batches(step, carry):
        cross_batch(2 * step + 1, crossed.at[1])
        finish_batch(2 * step, crossed.at[0])
        cross_batch(jnp.minimum(2 * step + 2, batches - 1), crossed.at[0])
        finish_batch(2 * step + 1, crossed.at[1])
        return carry

    cross_batch(0, crossed.at[0])
    lax.fori_loop(0, batches // 2, two_batches, 0)

    station_columns = stations_ref[...].T
    arrivals, masks = [], []
    for k in range(3):
        places = own_columns(place_windows.at[k])
        masks.append(own_columns(mask_windows.at[k]))
        _, distance = travel(places, station_columns)
        arrivals.append(places[3:4, :] + distance / WAVE_SPEED)
    near_arrivals, found = look_up(
        jnp.concatenate(arrivals, axis=1), jnp.concatenate(masks, axis=1), hits[...]
    )
    residual = (
        jnp.tile(masks[1], (1, K_HOME))
        * found
        * (by_pair(lag_ref[...], K_HOME) - (near_arrivals - jnp.tile(arrivals[1], (1, K_HOME))))
        * (1.0 / ((K_HOME + K_REGION) * stations))
    )
    own_sums = sum(residual[:, n * events : (n + 1) * events] for n in range(K_HOME))
    sums = sum_by_name(residual, hits[...])
    to_core_ref[...] = sums[:, :events]
    sums_ref[...] = own_sums - sums[:, events : 2 * events]
    to_x_ref[...] = sums[:, 2 * events :]


def pair_ids(id_rows, step, span):
    pieces = []
    for u in range(2):
        row = 4 * step + 2 * u
        pieces.append(id_rows[pl.ds(row, 1), :])
        pieces.append(id_rows[pl.ds(row + 1, 1), :][:, : span - LANES])
    return jnp.concatenate(pieces, axis=1)


def lookup_kernel(
    stations_ref,
    mine_ref,
    locations_ref,
    masks_ref,
    id_rows,
    found_ref,
    own_terms,
    place_window,
    mask_window,
    sems,
):
    sources, payload, _ = mine_ref.shape
    stations = sources // 2
    part = payload // COMPONENTS // 8 * 8
    events = 2 * part
    span = K_REGION * part
    width = 2 * span
    region_events = sources * events
    region, slab = lax.axis_index("region"), lax.axis_index("slab")
    core = region % 2
    task_region = region - core + slab // stations
    station = slab % stations
    columns = pl.ds(pl.multiple_of(task_region * region_events, region_events), region_events)
    copies = [
        pltpu.make_async_copy(locations_ref.at[:, columns], place_window, sems.at[0]),
        pltpu.make_async_copy(masks_ref.at[:, columns], mask_window, sems.at[1]),
    ]
    for copy in copies:
        copy.start()

    def read_ids(source, carry):
        tail = mine_ref[source, COMPONENTS * part :, :].astype(F32)
        rows = ((tail[:2] * events + tail[2:4]) * 8).astype(jnp.int32)
        id_rows[pl.ds(2 * source, 1), :] = rows[:1]
        id_rows[pl.ds(2 * source + 1, 1), :] = rows[1:]
        return carry

    lax.fori_loop(0, sources, read_ids, 0, unroll=8)
    for copy in copies:
        copy.wait()
    offsets = [place_window[c : c + 1, :] - stations_ref[c, station] for c in range(3)]
    arrival = place_window[3:4, :] + (
        jnp.sqrt(sum(offset * offset for offset in offsets)) / WAVE_SPEED
    )
    mask = mask_window[pl.ds(station, 1), :].astype(F32)

    def as_rows(row):
        return jnp.concatenate(
            [row[:, t * LANES : (t + 1) * LANES] for t in range(region_events // LANES)], axis=0
        )

    tables = jnp.concatenate(
        [part_of.astype(F32) for part_of in three_parts(as_rows(arrival))] + [as_rows(mask)], axis=0
    ).astype(BF16)
    half_rows = tables.shape[0] // 4
    lane = lax.broadcasted_iota(jnp.int32, (LANES, width), 1)
    event_rows = lax.broadcasted_iota(jnp.int32, (LANES, width), 0)
    own_hits = event_rows == lane // span * events + core * part + lane % part
    own_hits = jnp.where(own_hits, 1.0, 0.0).astype(BF16)
    own = jnp.dot(tables, own_hits, preferred_element_type=F32)
    own_terms[:half_rows] = own[:half_rows] + own[half_rows : 2 * half_rows] + own[
        2 * half_rows : 3 * half_rows
    ]
    own_terms[half_rows:] = own[3 * half_rows :]
    source_rows = lax.broadcasted_iota(jnp.int32, (half_rows, width), 0)

    def two_sources(step, carry):
        id_row = pair_ids(id_rows, step, span) // 8
        from_source = source_rows == id_row // LANES
        from_event = jnp.where(event_rows == id_row % LANES, 1.0, 0.0).astype(BF16)
        looked_up = jnp.dot(tables, from_event, preferred_element_type=F32)
        arrival = looked_up[:half_rows] + looked_up[half_rows : 2 * half_rows]
        arrival = arrival + looked_up[2 * half_rows : 3 * half_rows]
        mask = jnp.where(from_source, looked_up[3 * half_rows :], 0.0)
        found_ref[pl.ds(step, 1), :] = jnp.sum(
            jnp.where(from_source, arrival, 0.0), axis=0, keepdims=True
        )
        found_ref[pl.ds(half_rows + step, 1), :] = jnp.sum(mask, axis=0, keepdims=True)
        return carry

    lax.fori_loop(0, half_rows, two_sources, 0, unroll=4)


def task_kernel(
    id_rows,
    found_ref,
    own_terms,
    mine_ref,
    other_ref,
    turned_ref,
    out_ref,
    table,
    fetched_even,
    fetched_odd,
    crossed_even,
    crossed_odd,
    residuals,
    ids,
    sem,
):
    sources, payload, _ = mine_ref.shape
    stations = sources // 2
    part = payload // COMPONENTS // 8 * 8
    events = 2 * part
    span = K_REGION * part
    width = 2 * span
    core = lax.axis_index("region") % 2
    half_rows = sources // 2
    id_copy = pltpu.make_async_copy(id_rows, ids, sem)
    id_copy.start()

    def fill(source, carry):
        for ref, half in ((mine_ref, core), (other_ref, 1 - core)):
            rows = [
                ref[source, k * part : (k + 1) * part, :].astype(F32) for k in range(COMPONENTS)
            ]
            rows.append(swapped(rows[-1]))
            base = (source * events + half * part) * 8
            for k, values_k in enumerate(rows):
                table[pl.ds(base + k, part, stride=8), :] = values_k
                table[pl.ds(base + 4 + k, part, stride=8), :] = values_k
        return carry

    lax.fori_loop(0, sources, fill, 0, unroll=8)
    id_copy.wait()
    lane = lax.broadcasted_iota(jnp.int32, (LANES, width), 1)
    event_rows = lax.broadcasted_iota(jnp.int32, (LANES, width), 0)
    own_hits = event_rows == lane // span * events + core * part + lane % part
    own_hits = jnp.where(own_hits, 1.0, 0.0).astype(BF16)

    upper = lax.broadcasted_iota(jnp.int32, (8, LANES), 0) < 4
    source_rows = lax.broadcasted_iota(jnp.int32, (half_rows, width), 0)
    out_lane = lax.broadcasted_iota(jnp.int32, (1, LANES), 1)

    def fetch(step, into):
        for q in range(0, width, 2):
            row, column = q // span * 2 + q % span // LANES, q % span % LANES
            first = ids[step * 4 + row, column]
            second = ids[step * 4 + row, column + 1]
            first = table[pl.ds(pl.multiple_of(first, 8), 8), :]
            second = table[pl.ds(pl.multiple_of(second, 8), 8), :]
            into[q * 4 : q * 4 + 8, :] = jnp.where(upper, first, second)

    def cross_two(step, source, into):
        for u in range(2):
            own = multipliers(
                *(
                    mine_ref[2 * step + u, k * part : (k + 1) * part, :].astype(F32)
                    for k in range(COMPONENTS)
                )
            )
            for n in range(K_REGION):
                start = u * span + n * part
                partner = [
                    source[pl.ds(start * 4 + k, part, stride=4), :]
                    for k in range(COMPONENTS + 1)
                ]
                put_crossed(into, slice(start, start + part), own, partner)

    def finish(step, rows_ref, sums):
        lag = soft_lags_by_block(rows_ref, turned_ref)
        for u in range(2):
            rest = lag[:, u * span + LANES : (u + 1) * span]
            rest = jnp.concatenate([rest, jnp.zeros((1, LANES - rest.shape[1]), F32)], axis=1)
            out_ref[2 * step + u] = jnp.concatenate(
                [lag[:, u * span : u * span + LANES], rest], axis=0
            )
        id_row = pair_ids(id_rows, step, span) // 8
        from_source = source_rows == id_row // LANES
        from_event = jnp.where(event_rows == id_row % LANES, 1.0, 0.0).astype(BF16)
        arrival = found_ref[pl.ds(step, 1), :]
        mask = found_ref[pl.ds(half_rows + step, 1), :]
        residual = (
            own_terms[pl.ds(half_rows + step, 1), :]
            * mask
            * (lag - (arrival - own_terms[pl.ds(step, 1), :]))
            * (1.0 / ((K_LOCAL + K_REGION + K_CROSS) * stations))
        )
        residuals[pl.ds(step, 1), :] = residual
        terms = jnp.concatenate(two_parts(jnp.where(from_source, residual, 0.0)), axis=0)
        return sums + lax.dot_general(terms, from_event, BY_LAST, preferred_element_type=F32)

    steps = sources // 2

    def two_steps(pair, sums):
        first = 2 * pair
        fetch(jnp.minimum(first + 2, steps - 1), fetched_even)
        cross_two(first + 1, fetched_odd, crossed_odd)
        sums = finish(first, crossed_even, sums)
        fetch(jnp.minimum(first + 3, steps - 1), fetched_odd)
        cross_two(jnp.minimum(first + 2, steps - 1), fetched_even, crossed_even)
        return finish(first + 1, crossed_odd, sums)

    fetch(0, fetched_even)
    cross_two(0, fetched_even, crossed_even)
    fetch(1, fetched_odd)
    sums = lax.fori_loop(0, steps // 2, two_steps, jnp.zeros((2 * half_rows, LANES), F32))
    terms = jnp.concatenate(two_parts(residuals[...]), axis=0)
    sums = lax.dot_general(terms, own_hits, BY_LAST, preferred_element_type=F32) - sums
    sums = sums[:half_rows] + sums[half_rows:]
    for t in range(half_rows):
        for u in range(2):
            row = sums[t : t + 1, :]
            row = pltpu.roll(row, LANES // 2, 1) if u == 0 else row
            lags = out_ref[2 * t + u]
            out_ref[2 * t + u] = jnp.concatenate(
                [lags[:1], jnp.where(out_lane < span - LANES, lags[1:], row)], axis=0
            )


def gather_kernel(
    home_lag_ref,
    sums_ref,
    core_ref,
    x_ref,
    stations_ref,
    locations_ref,
    order_ref,
    lag_ref,
    last_ref,
    out_ref,
    direction_ref,
    place_window,
    sem,
):
    stations, events = sums_ref.shape
    copy = near_columns(locations_ref, place_window, sem, lax.axis_index("region"))
    local = K_LOCAL * stations
    remote = K_REGION * stations
    home = home_lag_ref[...]
    gap = jnp.zeros((events, remote), F32)
    last = jnp.concatenate([gap, home[:, local:]], axis=1)
    last_ref[...] = last
    lag_ref[...] = jnp.concatenate([home[:, :local], last], axis=1)
    out_ref[...] = sums_ref[...] - core_ref[...] - x_ref[...]
    copy.wait()
    offsets, distance = travel(own_columns(place_window), stations_ref[...].T)
    for c in range(3):
        direction_ref[c] = offsets[c] / (WAVE_SPEED * distance)


def final_kernel(
    kept_ref,
    got_ref,
    last_ref,
    sums_ref,
    direction_ref,
    home_lag_ref,
    lag_ref,
    grad_ref,
    lag_window,
    sem,
):
    events = grad_ref.shape[1]
    stations = sums_ref.shape[0]
    part = events // 2
    span = K_REGION * part
    core = lax.axis_index("region") % 2
    sums = sums_ref[...]
    block = pl.ds(pl.multiple_of(core * stations, stations), stations)
    kept, got = kept_ref[block], got_ref[block]
    rows = []
    for h in range(2):
        values = jnp.where(core == h, kept, got)
        sums = sums + values[:, 1, span - LANES :]
        turned = jnp.concatenate([values[:, 0, :], values[:, 1, : span - LANES]], axis=1).T
        rows.append(
            jnp.concatenate([turned[n * part : (n + 1) * part] for n in range(K_REGION)], axis=1)
        )
    rows = jnp.concatenate(rows, axis=0)
    lag_window[...] = jnp.concatenate([rows, last_ref[:, rows.shape[1] :]], axis=1)
    columns = pl.ds(K_LOCAL * stations, LANES)
    lags = pltpu.make_async_copy(lag_window, lag_ref.at[:, columns], sem)
    lags.start()
    for c in range(3):
        grad_ref[c : c + 1, :] = jnp.sum(direction_ref[c] * sums, axis=0, keepdims=True)
    grad_ref[3:4, :] = jnp.sum(sums, axis=0, keepdims=True)
    lags.wait()


def params(mebibytes):
    return pltpu.CompilerParams(vmem_limit_bytes=mebibytes * 1024 * 1024)


def vmem(count):
    return [pl.BlockSpec(memory_space=pltpu.VMEM)] * count


def smem(count):
    return [pl.BlockSpec(memory_space=pltpu.SMEM)] * count


def anywhere(count):
    return [pl.BlockSpec(memory_space=pl.ANY)] * count


def shape(dims, dtype=F32):
    return jax.ShapeDtypeStruct(dims, dtype)


def other_core(block):
    count = lax.axis_size("region")
    return lax.ppermute(block, "region", [(i, i + 1 - 2 * (i % 2)) for i in range(count)])


def other_chip(block):
    odd = range(1, lax.axis_size("region") - 1, 2)
    return lax.ppermute(block, "region", [p for i in odd for p in ((i, i + 1), (i + 1, i))])


def per_device(waveforms, neighbours, masks, locations, stations):
    events, channels, samples = waveforms.shape
    neighbour_count = neighbours.shape[1]
    station_count = stations.shape[1]
    slab_count = lax.axis_size("slab")
    region_events = slab_count * events
    core = lax.axis_index("region") % 2
    part = events // 2
    span = K_REGION * part
    inverse = jnp.asarray(inverse_rows(samples))
    turned = jnp.asarray(np.ascontiguousarray(inverse_rows(samples).T))
    wave_rows = waveforms.reshape(-1, samples)
    table = jnp.asarray(forward_table(samples))
    id_columns = neighbours.T
    by_event_shape = (events, COMPONENTS + 1, station_count, samples)
    payload_rows = COMPONENTS * part + 8

    kept, sent, by_event = pl.pallas_call(
        payload_kernel,
        out_shape=(
            shape((slab_count, payload_rows, samples), BF16),
            shape((station_count, payload_rows, samples), BF16),
            shape(by_event_shape, BF16),
        ),
        in_specs=vmem(3),
        out_specs=vmem(3),
        scratch_shapes=[pltpu.VMEM((events * channels, samples), F32)],
        compiler_params=params(60),
        name="payload",
    )(wave_rows, table, id_columns)
    payload = lax.dynamic_update_slice_in_dim(
        kept, other_core(sent), (1 - core) * station_count, 0
    )
    mine = lax.all_to_all(payload, "slab", 0, 0, tiled=True)

    core_spec = other_core(by_event)
    x_spec = other_chip(by_event)

    width = K_HOME * station_count
    lag_home, sums, to_core, to_x, done = pl.pallas_call(
        home_kernel,
        out_shape=(
            shape((events, width)),
            shape((station_count, events)),
            shape((station_count, events)),
            shape((station_count, events)),
            shape((1, 1, LANES), BF16),
        ),
        in_specs=smem(1) + vmem(3) + anywhere(5),
        out_specs=vmem(5),
        scratch_shapes=[
            pltpu.VMEM((3 * events, *by_event_shape[1:]), BF16),
            pltpu.VMEM((3 * events, *by_event_shape[1:]), F32),
            pltpu.VMEM((2, BATCH * width, COMPONENTS * samples), BF16),
            pltpu.VMEM((3 * events, K_HOME * events), BF16),
            pltpu.VMEM((3, 4, LANES), F32),
            pltpu.VMEM((3, station_count, LANES), jnp.int32),
            pltpu.SemaphoreType.DMA((9,)),
        ],
        compiler_params=params(26),
        cost_estimate=pl.CostEstimate(flops=10**10, bytes_accessed=10**7, transcendentals=10**7),
        name="home",
    )(
        id_columns,
        id_columns,
        stations,
        inverse,
        core_spec,
        by_event,
        x_spec,
        locations,
        masks,
    )
    from_core = other_core(to_core)
    from_x = other_chip(to_x)
    mine = lax.dynamic_update_slice(mine, done, (0, payload_rows - 1, 0))
    other = other_core(mine)

    id_rows, found, own_terms = pl.pallas_call(
        lookup_kernel,
        out_shape=(
            shape((2 * slab_count, LANES), jnp.int32),
            shape((slab_count, 2 * span)),
            shape((slab_count, 2 * span)),
        ),
        in_specs=smem(1) + vmem(1) + anywhere(2),
        out_specs=vmem(3),
        scratch_shapes=[
            pltpu.VMEM((4, region_events), F32),
            pltpu.VMEM((station_count, region_events), jnp.int32),
            pltpu.SemaphoreType.DMA((2,)),
        ],
        compiler_params=params(16),
        cost_estimate=pl.CostEstimate(flops=10**9, bytes_accessed=10**7, transcendentals=0),
        name="lookup",
    )(stations, mine, locations, masks)
    results = pl.pallas_call(
        task_kernel,
        out_shape=shape((slab_count, 2, LANES)),
        in_specs=vmem(6),
        out_specs=vmem(1)[0],
        scratch_shapes=[
            pltpu.VMEM((region_events * 8, LANES), F32),
            pltpu.VMEM((2 * span * 4, LANES), F32),
            pltpu.VMEM((2 * span * 4, LANES), F32),
            pltpu.VMEM((2 * span, COMPONENTS * samples), BF16),
            pltpu.VMEM((2 * span, COMPONENTS * samples), BF16),
            pltpu.VMEM((slab_count // 2, 2 * span), F32),
            pltpu.SMEM((2 * slab_count, LANES), jnp.int32),
            pltpu.SemaphoreType.DMA,
        ],
        compiler_params=params(26),
        cost_estimate=pl.CostEstimate(flops=10**10, bytes_accessed=10**7, transcendentals=10**7),
        name="task",
    )(id_rows, found, own_terms, mine, other, turned)
    back = lax.all_to_all(results, "slab", 0, 0, tiled=True)
    lag_home, last, sums, direction = pl.pallas_call(
        gather_kernel,
        out_shape=(
            shape((events, neighbour_count * station_count)),
            shape((events, LANES)),
            shape((station_count, events)),
            shape((3, station_count, events)),
        ),
        in_specs=vmem(5) + anywhere(2),
        out_specs=vmem(4),
        scratch_shapes=[pltpu.VMEM((4, LANES), F32), pltpu.SemaphoreType.DMA],
        compiler_params=params(8),
        cost_estimate=pl.CostEstimate(flops=10**9, bytes_accessed=10**7, transcendentals=0),
        name="gather",
    )(lag_home, sums, from_core, from_x, stations, locations, results)
    return pl.pallas_call(
        final_kernel,
        out_shape=(
            shape((events, neighbour_count * station_count)),
            shape((4, events)),
        ),
        in_specs=vmem(5) + anywhere(1),
        out_specs=(anywhere(1)[0], vmem(1)[0]),
        scratch_shapes=[pltpu.VMEM((events, LANES), F32), pltpu.SemaphoreType.DMA],
        input_output_aliases={5: 0},
        compiler_params=params(8),
        name="final",
    )(back, other_core(back), last, sums, direction, lag_home)


def solution(mesh):
    in_specs = (P(("region", "slab"), None, None), P(("region", "slab"), None), P(), P(), P())
    out_specs = (P(("region", "slab"), None), P(None, ("region", "slab")))
    return jax.shard_map(
        per_device, mesh=mesh, in_specs=in_specs, out_specs=out_specs, check_vma=False
    )
```

```python
import functools

import jax
import jax.numpy as jnp
import ml_dtypes
import numpy as np
from jax import lax
from jax.experimental import pallas as pl
from jax.experimental.pallas import tpu as pltpu
from jax.sharding import PartitionSpec as P

K_LOCAL = 24
K_REGION = 6
K_CROSS = 2
K_HOME = K_LOCAL + K_CROSS
COMPONENTS = 3
BATCH = 4
LANES = 128

SHARPNESS = 0.1
WAVE_SPEED = 0.6
EXPONENT_SCALE = SHARPNESS * 1.4426950408889634

F32 = jnp.float32
BF16 = jnp.bfloat16
BY_LAST = (((1,), (1,)), ((), ()))


def forward_table(samples):
    half_length = samples // 2
    sample_ids = np.arange(samples)[:, None]
    cos_bins = np.arange(half_length + 1)[None, :]
    sin_bins = np.arange(1, half_length)[None, :]
    cos_angle = 2.0 * np.pi / samples * (sample_ids * cos_bins % samples)
    sin_angle = 2.0 * np.pi / samples * (sample_ids * sin_bins % samples)
    table = np.concatenate([np.cos(cos_angle), -np.sin(sin_angle)], axis=1)
    return table.astype(np.float32).astype(ml_dtypes.bfloat16)


def inverse_table(samples):
    half_length = samples // 2
    cos_bins = np.arange(half_length + 1)[:, None]
    sin_bins = np.arange(1, half_length)[:, None]
    lag_ids = np.arange(samples)[None, :]
    factors = np.where((cos_bins == 0) | (cos_bins == half_length), 1.0, 2.0) / samples
    cos_angle = 2.0 * np.pi / samples * (cos_bins * lag_ids % samples)
    sin_angle = 2.0 * np.pi / samples * (sin_bins * lag_ids % samples)
    table = np.concatenate(
        [factors * np.cos(cos_angle), -(2.0 / samples) * np.sin(sin_angle)], axis=0
    )
    return table.astype(np.float32).astype(ml_dtypes.bfloat16)


def inverse_rows(samples):
    table = inverse_table(samples)
    real, imag = table[: samples // 2], table[samples // 2 :]
    return np.concatenate([real, real, imag, imag, table], axis=0)


def arrange(first, second):
    half = first.shape[-1] // 2
    lane = lax.broadcasted_iota(jnp.int32, first.shape, first.ndim - 1)
    real = jnp.where(lane < half, first, pltpu.roll(second, half, second.ndim - 1))
    imag = jnp.where(lane < half, pltpu.roll(first, half, first.ndim - 1), second)
    return real, imag


def swapped(spec):
    return pltpu.roll(spec, spec.shape[-1] // 2, spec.ndim - 1)


def multipliers(real, imag, packed):
    half = packed.shape[-1] // 2
    lane = lax.broadcasted_iota(jnp.int32, packed.shape, packed.ndim - 1)
    edge = (lane == 0) | (lane == half)
    turned = swapped(packed)
    packed_real = jnp.where(lane <= half, packed, turned)
    packed_imag = jnp.where(edge, 0.0, jnp.where(lane < half, turned, -packed))
    return real, jnp.where(edge, imag, real), jnp.where(edge, 0.0, imag), packed_real, packed_imag


def cross(own, partner):
    real, real_edge, imag, packed_real, packed_imag = own
    other_real, other_imag, other, other_swapped = partner
    return (
        real * other_real + imag * other_imag,
        real_edge * other_imag - imag * other_real,
        packed_real * other + packed_imag * other_swapped,
    )


def soft_lags(corr):
    top = jnp.max(corr, axis=0, keepdims=True)
    weights = jnp.exp2((corr - top) * EXPONENT_SCALE)
    groups = [weights[k : k + 8] for k in range(0, weights.shape[0], 8)]
    half = len(groups) // 2
    after = groups[half - 1]
    ahead = after
    for k in range(half - 2, 0, -1):
        after = after + groups[k]
        ahead = ahead + after
    after = after + groups[0]
    before = groups[half]
    behind = before
    for k in range(half + 1, len(groups)):
        before = before + groups[k]
        behind = behind + before
    total = after + before
    row = lax.broadcasted_iota(jnp.int32, total.shape, 0).astype(F32)
    moment = jnp.sum((ahead - behind) * 8.0 + row * total, axis=0, keepdims=True)
    return moment / jnp.sum(total, axis=0, keepdims=True)


def all_soft_lags(crossed_ref, inverse_ref):
    corr = jnp.dot(crossed_ref[...], inverse_ref[...], preferred_element_type=F32)
    lags = [soft_lags(corr[k : k + LANES].T) for k in range(0, corr.shape[0], LANES)]
    return jnp.concatenate(lags, axis=1)


def soft_lags_by_block(crossed_ref, turned_ref):
    lags = []
    corr = lax.dot_general(turned_ref[...], crossed_ref[...], BY_LAST, preferred_element_type=F32)
    for k in range(0, crossed_ref.shape[0], LANES):
        lags.append(soft_lags(corr[:, k : k + LANES]))
    return jnp.concatenate(lags, axis=1)


def two_parts(x):
    high = x.astype(BF16)
    return high, (x - high.astype(F32)).astype(BF16)


def transform(wave_ref, table_ref, scr):
    block = 384

    def step(k, carry):
        rows = pl.ds(pl.multiple_of(k * block, block), block)
        spec = jnp.dot(wave_ref[rows, :], table_ref[...], preferred_element_type=F32)
        scr[rows, :] = spec.astype(BF16).astype(F32)
        return carry

    lax.fori_loop(0, wave_ref.shape[0] // block, step, 0, unroll=True)


def near_columns(ref, window, sem, region):
    slab = lax.axis_index("slab")
    start = region * (lax.axis_size("slab") * LANES // 2) + slab // 2 * LANES
    copy = pltpu.make_async_copy(
        ref.at[:, pl.ds(pl.multiple_of(start, LANES), LANES)], window, sem
    )
    copy.start()
    return copy


def own_columns(window):
    odd = lax.axis_index("slab") % 2 == 1
    values = window[...].astype(F32)
    half = values.shape[1] // 2
    return jnp.where(odd, pltpu.roll(values, half, 1), values)[:, :half]


def travel(places, station_columns):
    offsets = [places[c : c + 1, :] - station_columns[:, c : c + 1] for c in range(3)]
    return offsets, jnp.sqrt(sum(offset * offset for offset in offsets))


def three_parts(x):
    high = x.astype(BF16)
    rest = x - high.astype(F32)
    middle = rest.astype(BF16)
    return high, middle, (rest - middle.astype(F32)).astype(BF16)


def put_crossed(crossed, rows, own, partner):
    for k, values in enumerate(cross(own, partner)):
        crossed[rows, k * LANES : (k + 1) * LANES] = values.astype(BF16)


def look_up(arrival, mask, hits):
    stations = arrival.shape[0]
    rows = jnp.concatenate([p.astype(F32) for p in three_parts(arrival)] + [mask], axis=0)
    rows = jnp.dot(rows.astype(BF16), hits, preferred_element_type=F32)
    high, middle, low, found = (rows[k * stations : (k + 1) * stations] for k in range(4))
    return high + middle + low, found


def sum_by_name(residual, hits):
    stations = residual.shape[0]
    parts = jnp.concatenate(two_parts(residual), axis=0)
    sums = lax.dot_general(parts, hits, BY_LAST, preferred_element_type=F32)
    return sums[:stations] + sums[stations:]


def by_pair(lags, columns):
    turned = lags.T
    stations = turned.shape[0] // columns
    return jnp.concatenate(
        [turned[n * stations : (n + 1) * stations] for n in range(columns)], axis=1
    )


def payload_kernel(wave_ref, table_ref, ids_ref, kept_ref, sent_ref, by_event_ref, scr):
    stations = sent_ref.shape[0]
    events = ids_ref.shape[1]
    part = events // 2
    channels = stations * COMPONENTS
    core = lax.axis_index("region") % 2
    transform(wave_ref, table_ref, scr)
    ids = ids_ref[K_LOCAL : K_LOCAL + K_REGION, :]
    tail = sent_ref.shape[1] - COMPONENTS * part
    for out, base, half in ((kept_ref, core * stations, core), (sent_ref, 0, 1 - core)):
        mine = jnp.where(half == 1, ids[:, part:], ids[:, :part])
        row = jnp.concatenate([mine[n : n + 1] for n in range(K_REGION)], axis=1)
        row = jnp.concatenate([row, jnp.zeros((1, 2 * LANES - row.shape[1]), jnp.int32)], axis=1)
        source, event = row // events % (2 * stations), row % events
        rows = jnp.concatenate(
            [source[:, :LANES], source[:, LANES:], event[:, :LANES], event[:, LANES:]]
            + [jnp.zeros((tail - 4, LANES), jnp.int32)],
            axis=0,
        )
        rows = rows.astype(F32).astype(BF16)
        for s in range(stations):
            first, second, third = (
                scr[pl.ds(half * (part * channels) + COMPONENTS * s + c, part, stride=channels), :]
                for c in range(COMPONENTS)
            )
            for k, values in enumerate((*arrange(first, second), third)):
                out[base + s, k * part : (k + 1) * part, :] = values.astype(BF16)
            out[base + s, COMPONENTS * part :, :] = rows

    def one_event(event, carry):
        first, second, third = (
            scr[pl.ds(event * channels + c, stations, stride=COMPONENTS), :]
            for c in range(COMPONENTS)
        )
        for k, values in enumerate((*arrange(first, second), third, swapped(third))):
            by_event_ref[event, k] = values.astype(BF16)
        return carry

    lax.fori_loop(0, events, one_event, 0, unroll=8)


def home_kernel(
    ids,
    id_ref,
    stations_ref,
    inverse_ref,
    core_ref,
    own_ref,
    x_ref,
    locations_ref,
    masks_ref,
    lag_ref,
    sums_ref,
    to_core_ref,
    to_x_ref,
    done_ref,
    raw,
    pool,
    crossed,
    hits,
    place_windows,
    mask_windows,
    sems,
):
    events, _, stations, _ = own_ref.shape
    width = K_HOME * stations
    batches = events // BATCH
    region = lax.axis_index("region")
    last = lax.axis_size("region") - 1
    copies = [
        pltpu.make_async_copy(ref, raw.at[pl.ds(k * events, events)], sems.at[k])
        for k, ref in enumerate((core_ref, own_ref, x_ref))
    ]
    for copy in copies:
        copy.start()
    odd = region % 2
    near = (region + 1 - 2 * odd, region, jnp.clip(region - 1 + 2 * odd, 0, last))
    for k, where in enumerate(near):
        copies.append(near_columns(locations_ref, place_windows.at[k], sems.at[3 + k], where))
        copies.append(near_columns(masks_ref, mask_windows.at[k], sems.at[6 + k], where))
    blocks = [events] * K_LOCAL + [
        jnp.where((odd == 1) | (region == 0), 0, 2 * events),
        jnp.where((odd == 0) | (region == last), 0, 2 * events),
    ]
    columns = [*range(K_LOCAL), *range(K_LOCAL + K_REGION, K_LOCAL + K_REGION + K_CROSS)]
    named = lax.broadcasted_iota(jnp.int32, (3 * events, events), 0)
    for n in range(0, K_HOME, 2):
        pair = [
            jnp.where(
                id_ref[columns[m] : columns[m] + 1, :] % events + blocks[m] == named, 1.0, 0.0
            )
            for m in (n, n + 1)
        ]
        hits[:, n * events : (n + 2) * events] = jnp.concatenate(pair, axis=1).astype(BF16)
    done_ref[...] = jnp.zeros(done_ref.shape, done_ref.dtype)
    for copy in copies:
        copy.wait()

    def widen(event, carry):
        pool[event] = raw[event].astype(F32)
        return carry

    lax.fori_loop(0, 3 * events, widen, 0, unroll=8)

    def cross_batch(batch, rows_ref):
        for b in range(BATCH):
            event = batch * BATCH + b
            own = multipliers(*(pool[events + event, k] for k in range(COMPONENTS)))
            for n in range(K_HOME):
                j = lax.bitwise_and(ids[columns[n], event], events - 1) + blocks[n]
                partner = [pool[j, k] for k in range(COMPONENTS + 1)]
                start = b * width + n * stations
                put_crossed(rows_ref, slice(start, start + stations), own, partner)

    def finish_batch(batch, rows_ref):
        lags = all_soft_lags(rows_ref, inverse_ref)
        for b in range(BATCH):
            lag_ref[pl.ds(batch * BATCH + b, 1), :] = lags[:, b * width : (b + 1) * width]

    def two_batches(step, carry):
        cross_batch(2 * step + 1, crossed.at[1])
        finish_batch(2 * step, crossed.at[0])
        cross_batch(jnp.minimum(2 * step + 2, batches - 1), crossed.at[0])
        finish_batch(2 * step + 1, crossed.at[1])
        return carry

    cross_batch(0, crossed.at[0])
    lax.fori_loop(0, batches // 2, two_batches, 0)

    station_columns = stations_ref[...].T
    arrivals, masks = [], []
    for k in range(3):
        places = own_columns(place_windows.at[k])
        masks.append(own_columns(mask_windows.at[k]))
        _, distance = travel(places, station_columns)
        arrivals.append(places[3:4, :] + distance / WAVE_SPEED)
    near_arrivals, found = look_up(
        jnp.concatenate(arrivals, axis=1), jnp.concatenate(masks, axis=1), hits[...]
    )
    residual = (
        jnp.tile(masks[1], (1, K_HOME))
        * found
        * (by_pair(lag_ref[...], K_HOME) - (near_arrivals - jnp.tile(arrivals[1], (1, K_HOME))))
        * (1.0 / ((K_HOME + K_REGION) * stations))
    )
    own_sums = sum(residual[:, n * events : (n + 1) * events] for n in range(K_HOME))
    sums = sum_by_name(residual, hits[...])
    to_core_ref[...] = sums[:, :events]
    sums_ref[...] = own_sums - sums[:, events : 2 * events]
    to_x_ref[...] = sums[:, 2 * events :]


def pair_ids(id_rows, step, span):
    pieces = []
    for u in range(2):
        row = 4 * step + 2 * u
        pieces.append(id_rows[pl.ds(row, 1), :])
        pieces.append(id_rows[pl.ds(row + 1, 1), :][:, : span - LANES])
    return jnp.concatenate(pieces, axis=1)


def lookup_kernel(
    stations_ref,
    mine_ref,
    locations_ref,
    masks_ref,
    id_rows,
    found_ref,
    own_terms,
    place_window,
    mask_window,
    sems,
):
    sources, payload, _ = mine_ref.shape
    stations = sources // 2
    part = payload // COMPONENTS // 8 * 8
    events = 2 * part
    span = K_REGION * part
    width = 2 * span
    region_events = sources * events
    region, slab = lax.axis_index("region"), lax.axis_index("slab")
    core = region % 2
    task_region = region - core + slab // stations
    station = slab % stations
    columns = pl.ds(pl.multiple_of(task_region * region_events, region_events), region_events)
    copies = [
        pltpu.make_async_copy(locations_ref.at[:, columns], place_window, sems.at[0]),
        pltpu.make_async_copy(masks_ref.at[:, columns], mask_window, sems.at[1]),
    ]
    for copy in copies:
        copy.start()

    def read_ids(source, carry):
        tail = mine_ref[source, COMPONENTS * part :, :].astype(F32)
        rows = ((tail[:2] * events + tail[2:4]) * 8).astype(jnp.int32)
        id_rows[pl.ds(2 * source, 1), :] = rows[:1]
        id_rows[pl.ds(2 * source + 1, 1), :] = rows[1:]
        return carry

    lax.fori_loop(0, sources, read_ids, 0, unroll=8)
    for copy in copies:
        copy.wait()
    offsets = [place_window[c : c + 1, :] - stations_ref[c, station] for c in range(3)]
    arrival = place_window[3:4, :] + (
        jnp.sqrt(sum(offset * offset for offset in offsets)) / WAVE_SPEED
    )
    mask = mask_window[pl.ds(station, 1), :].astype(F32)

    def as_rows(row):
        return jnp.concatenate(
            [row[:, t * LANES : (t + 1) * LANES] for t in range(region_events // LANES)], axis=0
        )

    tables = jnp.concatenate(
        [part_of.astype(F32) for part_of in three_parts(as_rows(arrival))] + [as_rows(mask)], axis=0
    ).astype(BF16)
    half_rows = tables.shape[0] // 4
    lane = lax.broadcasted_iota(jnp.int32, (LANES, width), 1)
    event_rows = lax.broadcasted_iota(jnp.int32, (LANES, width), 0)
    own_hits = event_rows == lane // span * events + core * part + lane % part
    own_hits = jnp.where(own_hits, 1.0, 0.0).astype(BF16)
    own = jnp.dot(tables, own_hits, preferred_element_type=F32)
    own_terms[:half_rows] = own[:half_rows] + own[half_rows : 2 * half_rows] + own[
        2 * half_rows : 3 * half_rows
    ]
    own_terms[half_rows:] = own[3 * half_rows :]
    source_rows = lax.broadcasted_iota(jnp.int32, (half_rows, width), 0)

    def two_sources(step, carry):
        id_row = pair_ids(id_rows, step, span) // 8
        from_source = source_rows == id_row // LANES
        from_event = jnp.where(event_rows == id_row % LANES, 1.0, 0.0).astype(BF16)
        looked_up = jnp.dot(tables, from_event, preferred_element_type=F32)
        arrival = looked_up[:half_rows] + looked_up[half_rows : 2 * half_rows]
        arrival = arrival + looked_up[2 * half_rows : 3 * half_rows]
        mask = jnp.where(from_source, looked_up[3 * half_rows :], 0.0)
        found_ref[pl.ds(step, 1), :] = jnp.sum(
            jnp.where(from_source, arrival, 0.0), axis=0, keepdims=True
        )
        found_ref[pl.ds(half_rows + step, 1), :] = jnp.sum(mask, axis=0, keepdims=True)
        return carry

    lax.fori_loop(0, half_rows, two_sources, 0, unroll=4)


def task_kernel(
    id_rows,
    found_ref,
    own_terms,
    mine_ref,
    other_ref,
    turned_ref,
    out_ref,
    table,
    fetched_even,
    fetched_odd,
    crossed_even,
    crossed_odd,
    residuals,
    ids,
    sem,
):
    sources, payload, _ = mine_ref.shape
    stations = sources // 2
    part = payload // COMPONENTS // 8 * 8
    events = 2 * part
    span = K_REGION * part
    width = 2 * span
    core = lax.axis_index("region") % 2
    half_rows = sources // 2
    id_copy = pltpu.make_async_copy(id_rows, ids, sem)
    id_copy.start()

    def fill(source, carry):
        for ref, half in ((mine_ref, core), (other_ref, 1 - core)):
            rows = [
                ref[source, k * part : (k + 1) * part, :].astype(F32) for k in range(COMPONENTS)
            ]
            rows.append(swapped(rows[-1]))
            base = (source * events + half * part) * 8
            for k, values_k in enumerate(rows):
                table[pl.ds(base + k, part, stride=8), :] = values_k
                table[pl.ds(base + 4 + k, part, stride=8), :] = values_k
        return carry

    lax.fori_loop(0, sources, fill, 0, unroll=8)
    id_copy.wait()
    lane = lax.broadcasted_iota(jnp.int32, (LANES, width), 1)
    event_rows = lax.broadcasted_iota(jnp.int32, (LANES, width), 0)
    own_hits = event_rows == lane // span * events + core * part + lane % part
    own_hits = jnp.where(own_hits, 1.0, 0.0).astype(BF16)

    upper = lax.broadcasted_iota(jnp.int32, (8, LANES), 0) < 4
    source_rows = lax.broadcasted_iota(jnp.int32, (half_rows, width), 0)
    out_lane = lax.broadcasted_iota(jnp.int32, (1, LANES), 1)

    def fetch(step, into):
        for q in range(0, width, 2):
            row, column = q // span * 2 + q % span // LANES, q % span % LANES
            first = ids[step * 4 + row, column]
            second = ids[step * 4 + row, column + 1]
            first = table[pl.ds(pl.multiple_of(first, 8), 8), :]
            second = table[pl.ds(pl.multiple_of(second, 8), 8), :]
            into[q * 4 : q * 4 + 8, :] = jnp.where(upper, first, second)

    def cross_two(step, source, into):
        for u in range(2):
            own = multipliers(
                *(
                    mine_ref[2 * step + u, k * part : (k + 1) * part, :].astype(F32)
                    for k in range(COMPONENTS)
                )
            )
            for n in range(K_REGION):
                start = u * span + n * part
                partner = [
                    source[pl.ds(start * 4 + k, part, stride=4), :]
                    for k in range(COMPONENTS + 1)
                ]
                put_crossed(into, slice(start, start + part), own, partner)

    def finish(step, rows_ref, sums):
        lag = soft_lags_by_block(rows_ref, turned_ref)
        for u in range(2):
            rest = lag[:, u * span + LANES : (u + 1) * span]
            rest = jnp.concatenate([rest, jnp.zeros((1, LANES - rest.shape[1]), F32)], axis=1)
            out_ref[2 * step + u] = jnp.concatenate(
                [lag[:, u * span : u * span + LANES], rest], axis=0
            )
        id_row = pair_ids(id_rows, step, span) // 8
        from_source = source_rows == id_row // LANES
        from_event = jnp.where(event_rows == id_row % LANES, 1.0, 0.0).astype(BF16)
        arrival = found_ref[pl.ds(step, 1), :]
        mask = found_ref[pl.ds(half_rows + step, 1), :]
        residual = (
            own_terms[pl.ds(half_rows + step, 1), :]
            * mask
            * (lag - (arrival - own_terms[pl.ds(step, 1), :]))
            * (1.0 / ((K_LOCAL + K_REGION + K_CROSS) * stations))
        )
        residuals[pl.ds(step, 1), :] = residual
        terms = jnp.concatenate(two_parts(jnp.where(from_source, residual, 0.0)), axis=0)
        return sums + lax.dot_general(terms, from_event, BY_LAST, preferred_element_type=F32)

    steps = sources // 2

    def two_steps(pair, sums):
        first = 2 * pair
        fetch(jnp.minimum(first + 2, steps - 1), fetched_even)
        cross_two(first + 1, fetched_odd, crossed_odd)
        sums = finish(first, crossed_even, sums)
        fetch(jnp.minimum(first + 3, steps - 1), fetched_odd)
        cross_two(jnp.minimum(first + 2, steps - 1), fetched_even, crossed_even)
        return finish(first + 1, crossed_odd, sums)

    fetch(0, fetched_even)
    cross_two(0, fetched_even, crossed_even)
    fetch(1, fetched_odd)
    sums = lax.fori_loop(0, steps // 2, two_steps, jnp.zeros((2 * half_rows, LANES), F32))
    terms = jnp.concatenate(two_parts(residuals[...]), axis=0)
    sums = lax.dot_general(terms, own_hits, BY_LAST, preferred_element_type=F32) - sums
    sums = sums[:half_rows] + sums[half_rows:]
    for t in range(half_rows):
        for u in range(2):
            row = sums[t : t + 1, :]
            row = pltpu.roll(row, LANES // 2, 1) if u == 0 else row
            lags = out_ref[2 * t + u]
            out_ref[2 * t + u] = jnp.concatenate(
                [lags[:1], jnp.where(out_lane < span - LANES, lags[1:], row)], axis=0
            )


def gather_kernel(
    home_lag_ref,
    sums_ref,
    core_ref,
    x_ref,
    stations_ref,
    locations_ref,
    order_ref,
    lag_ref,
    last_ref,
    out_ref,
    direction_ref,
    place_window,
    sem,
):
    stations, events = sums_ref.shape
    copy = near_columns(locations_ref, place_window, sem, lax.axis_index("region"))
    local = K_LOCAL * stations
    remote = K_REGION * stations
    home = home_lag_ref[...]
    gap = jnp.zeros((events, remote), F32)
    last = jnp.concatenate([gap, home[:, local:]], axis=1)
    last_ref[...] = last
    lag_ref[...] = jnp.concatenate([home[:, :local], last], axis=1)
    out_ref[...] = sums_ref[...] - core_ref[...] - x_ref[...]
    copy.wait()
    offsets, distance = travel(own_columns(place_window), stations_ref[...].T)
    for c in range(3):
        direction_ref[c] = offsets[c] / (WAVE_SPEED * distance)


def final_kernel(
    kept_ref,
    got_ref,
    last_ref,
    sums_ref,
    direction_ref,
    home_lag_ref,
    lag_ref,
    grad_ref,
    lag_window,
    sem,
):
    events = grad_ref.shape[1]
    stations = sums_ref.shape[0]
    part = events // 2
    span = K_REGION * part
    core = lax.axis_index("region") % 2
    sums = sums_ref[...]
    block = pl.ds(pl.multiple_of(core * stations, stations), stations)
    kept, got = kept_ref[block], got_ref[block]
    rows = []
    for h in range(2):
        values = jnp.where(core == h, kept, got)
        sums = sums + values[:, 1, span - LANES :]
        turned = jnp.concatenate([values[:, 0, :], values[:, 1, : span - LANES]], axis=1).T
        rows.append(
            jnp.concatenate([turned[n * part : (n + 1) * part] for n in range(K_REGION)], axis=1)
        )
    rows = jnp.concatenate(rows, axis=0)
    lag_window[...] = jnp.concatenate([rows, last_ref[:, rows.shape[1] :]], axis=1)
    columns = pl.ds(K_LOCAL * stations, LANES)
    lags = pltpu.make_async_copy(lag_window, lag_ref.at[:, columns], sem)
    lags.start()
    for c in range(3):
        grad_ref[c : c + 1, :] = jnp.sum(direction_ref[c] * sums, axis=0, keepdims=True)
    grad_ref[3:4, :] = jnp.sum(sums, axis=0, keepdims=True)
    lags.wait()


def params(mebibytes):
    return pltpu.CompilerParams(vmem_limit_bytes=mebibytes * 1024 * 1024)


def vmem(count):
    return [pl.BlockSpec(memory_space=pltpu.VMEM)] * count


def smem(count):
    return [pl.BlockSpec(memory_space=pltpu.SMEM)] * count


def anywhere(count):
    return [pl.BlockSpec(memory_space=pl.ANY)] * count


def shape(dims, dtype=F32):
    return jax.ShapeDtypeStruct(dims, dtype)


def other_core(block):
    count = lax.axis_size("region")
    return lax.ppermute(block, "region", [(i, i + 1 - 2 * (i % 2)) for i in range(count)])


def other_chip(block):
    odd = range(1, lax.axis_size("region") - 1, 2)
    return lax.ppermute(block, "region", [p for i in odd for p in ((i, i + 1), (i + 1, i))])


def per_device(waveforms, neighbours, masks, locations, stations):
    events, channels, samples = waveforms.shape
    neighbour_count = neighbours.shape[1]
    station_count = stations.shape[1]
    slab_count = lax.axis_size("slab")
    region_events = slab_count * events
    core = lax.axis_index("region") % 2
    part = events // 2
    span = K_REGION * part
    inverse = jnp.asarray(inverse_rows(samples))
    turned = jnp.asarray(np.ascontiguousarray(inverse_rows(samples).T))
    wave_rows = waveforms.reshape(-1, samples)
    table = jnp.asarray(forward_table(samples))
    id_columns = neighbours.T
    by_event_shape = (events, COMPONENTS + 1, station_count, samples)
    payload_rows = COMPONENTS * part + 8

    kept, sent, by_event = pl.pallas_call(
        payload_kernel,
        out_shape=(
            shape((slab_count, payload_rows, samples), BF16),
            shape((station_count, payload_rows, samples), BF16),
            shape(by_event_shape, BF16),
        ),
        in_specs=vmem(3),
        out_specs=vmem(3),
        scratch_shapes=[pltpu.VMEM((events * channels, samples), F32)],
        compiler_params=params(60),
        name="payload",
    )(wave_rows, table, id_columns)
    payload = lax.dynamic_update_slice_in_dim(
        kept, other_core(sent), (1 - core) * station_count, 0
    )
    mine = lax.all_to_all(payload, "slab", 0, 0, tiled=True)

    core_spec = other_core(by_event)
    x_spec = other_chip(by_event)

    width = K_HOME * station_count
    lag_home, sums, to_core, to_x, done = pl.pallas_call(
        home_kernel,
        out_shape=(
            shape((events, width)),
            shape((station_count, events)),
            shape((station_count, events)),
            shape((station_count, events)),
            shape((1, 1, LANES), BF16),
        ),
        in_specs=smem(1) + vmem(3) + anywhere(5),
        out_specs=vmem(5),
        scratch_shapes=[
            pltpu.VMEM((3 * events, *by_event_shape[1:]), BF16),
            pltpu.VMEM((3 * events, *by_event_shape[1:]), F32),
            pltpu.VMEM((2, BATCH * width, COMPONENTS * samples), BF16),
            pltpu.VMEM((3 * events, K_HOME * events), BF16),
            pltpu.VMEM((3, 4, LANES), F32),
            pltpu.VMEM((3, station_count, LANES), jnp.int32),
            pltpu.SemaphoreType.DMA((9,)),
        ],
        compiler_params=params(26),
        cost_estimate=pl.CostEstimate(flops=10**10, bytes_accessed=10**7, transcendentals=10**7),
        name="home",
    )(
        id_columns,
        id_columns,
        stations,
        inverse,
        core_spec,
        by_event,
        x_spec,
        locations,
        masks,
    )
    from_core = other_core(to_core)
    from_x = other_chip(to_x)
    mine = lax.dynamic_update_slice(mine, done, (0, payload_rows - 1, 0))
    other = other_core(mine)

    id_rows, found, own_terms = pl.pallas_call(
        lookup_kernel,
        out_shape=(
            shape((2 * slab_count, LANES), jnp.int32),
            shape((slab_count, 2 * span)),
            shape((slab_count, 2 * span)),
        ),
        in_specs=smem(1) + vmem(1) + anywhere(2),
        out_specs=vmem(3),
        scratch_shapes=[
            pltpu.VMEM((4, region_events), F32),
            pltpu.VMEM((station_count, region_events), jnp.int32),
            pltpu.SemaphoreType.DMA((2,)),
        ],
        compiler_params=params(16),
        cost_estimate=pl.CostEstimate(flops=10**9, bytes_accessed=10**7, transcendentals=0),
        name="lookup",
    )(stations, mine, locations, masks)
    results = pl.pallas_call(
        task_kernel,
        out_shape=shape((slab_count, 2, LANES)),
        in_specs=vmem(6),
        out_specs=vmem(1)[0],
        scratch_shapes=[
            pltpu.VMEM((region_events * 8, LANES), F32),
            pltpu.VMEM((2 * span * 4, LANES), F32),
            pltpu.VMEM((2 * span * 4, LANES), F32),
            pltpu.VMEM((2 * span, COMPONENTS * samples), BF16),
            pltpu.VMEM((2 * span, COMPONENTS * samples), BF16),
            pltpu.VMEM((slab_count // 2, 2 * span), F32),
            pltpu.SMEM((2 * slab_count, LANES), jnp.int32),
            pltpu.SemaphoreType.DMA,
        ],
        compiler_params=params(26),
        cost_estimate=pl.CostEstimate(flops=10**10, bytes_accessed=10**7, transcendentals=10**7),
        name="task",
    )(id_rows, found, own_terms, mine, other, turned)
    back = lax.all_to_all(results, "slab", 0, 0, tiled=True)
    lag_home, last, sums, direction = pl.pallas_call(
        gather_kernel,
        out_shape=(
            shape((events, neighbour_count * station_count)),
            shape((events, LANES)),
            shape((station_count, events)),
            shape((3, station_count, events)),
        ),
        in_specs=vmem(5) + anywhere(2),
        out_specs=vmem(4),
        scratch_shapes=[pltpu.VMEM((4, LANES), F32), pltpu.SemaphoreType.DMA],
        compiler_params=params(8),
        cost_estimate=pl.CostEstimate(flops=10**9, bytes_accessed=10**7, transcendentals=0),
        name="gather",
    )(lag_home, sums, from_core, from_x, stations, locations, results)
    return pl.pallas_call(
        final_kernel,
        out_shape=(
            shape((events, neighbour_count * station_count)),
            shape((4, events)),
        ),
        in_specs=vmem(5) + anywhere(1),
        out_specs=(anywhere(1)[0], vmem(1)[0]),
        scratch_shapes=[pltpu.VMEM((events, LANES), F32), pltpu.SemaphoreType.DMA],
        input_output_aliases={5: 0},
        compiler_params=params(8),
        name="final",
    )(back, other_core(back), last, sums, direction, lag_home)


def solution(mesh):
    in_specs = (P(("region", "slab"), None, None), P(("region", "slab"), None), P(), P(), P())
    out_specs = (P(("region", "slab"), None), P(None, ("region", "slab")))
    return jax.shard_map(
        per_device, mesh=mesh, in_specs=in_specs, out_specs=out_specs, check_vma=False
    )
```
